256 devices in a mesh: section: 2 (over z_lo), shard: 64 (over y, x, z_hi), rep: 2 (over core).
Axes of the slice: x: 4, y: 4, z: 8 (z_hi: 4, z_lo: 2; z = z_hi * 2 + z_lo), core: 2. Of those that a mesh axis runs over, the one named last changes fastest.
Arguments:
- acts: bfloat16 [2, 2, 1536, 4608], P('section', 'rep', 'shard'), may hold values from -6 to 6
- logit_grad: bfloat16 [2, 1536, 24576], P('rep', None, 'shard'), may hold values from -0.109375 to 0.109375
- token_ids: int32 [2, 1536], P('rep'), may hold values from 0 to 255999
- table: float32 [24576, 4608], P(('shard', 'section', 'rep')), may hold values from -4 to 4
- moment_one: float32 [24576, 4608], P(('shard', 'section', 'rep')), may hold values from -3 to 3
- moment_two: float32 [24576, 4608], P(('shard', 'section', 'rep')), may hold values from 0.05 to 2
Outputs:
- new_table: float32 [24576, 4608], P(('shard', 'section', 'rep'))
- new_moment_one: float32 [24576, 4608], P(('shard', 'section', 'rep'))
- new_moment_two: float32 [24576, 4608], P(('shard', 'section', 'rep'))
The draws below stay inside these ranges and needn't reach their ends.
All inputs are finite; a program needn't handle non-finite values.
Results may differ from the reference program's by a relative error of at most 0.0003.
Values may be sent and summed in bfloat16 or wider, within the bound.
No kernel may reach another device: no remote copies, remote signals or barrier semaphores. Data moves between devices by JAX's collectives and lax.ppermute only.
A program may use at most 128 MiB of HBM per device.

```python
import math
import jax
import jax.numpy as jnp
from jax import lax

D = 4608
VOCAB = 24576
TOK_REP = 1536
REPS = 2
SECTIONS = 2
TOKENS = 3072


def plant(result, stream_key, smallest, largest):
    shape = result.shape
    place = [jax.random.randint(jax.random.fold_in(stream_key, axis), (), 0, shape[axis]) for axis in range(len(shape))]
    result = result.at[tuple(place)].set(smallest)
    longest = shape.index(max(shape))
    place[longest] = (place[longest] + 1) % shape[longest]
    return result.at[tuple(place)].set(largest)


def block_levels(own_key, extent, shards, smallest, largest):
    loudness = 1.0
    for position, blocks in shards:
        steps = jax.random.uniform(jax.random.fold_in(jax.random.fold_in(own_key, 6), position), (blocks,), jnp.float32, smallest / len(shards), largest / len(shards))
        loudness = loudness * jnp.repeat(jnp.exp(steps), extent[position] // blocks).reshape((-1,) + (1,) * (len(extent) - 1 - position))
    return loudness


def gaussian(own_key, dims, deviation, most, split=(), kind=jnp.bfloat16):
    array = deviation * jax.random.normal(own_key, dims, jnp.float32)
    if split:
        array = array * block_levels(own_key, dims, split, -0.22, 0.18)
    return jnp.clip(array, -most, most).astype(kind)


def setup_inputs(seed: int = 0) -> dict:
    key_list = jax.random.split(jax.random.key(seed), 7)
    acts = gaussian(key_list[0], (SECTIONS, REPS, TOK_REP, D), 1.0, 6.0, ((0, 2), (1, 2), (2, 64)))
    logit_grad = gaussian(key_list[1], (REPS, TOK_REP, VOCAB), TOKENS ** -0.5, 0.109375, ((0, 2), (2, 64)))
    token_ids = plant(jax.random.randint(key_list[2], (REPS, TOK_REP), 0, VOCAB * 125 // 12), jax.random.fold_in(key_list[2], 1), 0, (VOCAB * 125 // 12) - 1).astype(jnp.int32)
    table = gaussian(key_list[3], (VOCAB, D), 0.5, 4.0, ((0, 256),), jnp.float32)
    moment_one = gaussian(key_list[4], (VOCAB, D), 0.3, 3.0, ((0, 256),), jnp.float32)
    moment_two = jnp.clip(jnp.exp(math.log(2.0) - 3.6888794 * jax.random.uniform(key_list[5], (VOCAB, D), jnp.float32) ** block_levels(key_list[5], (VOCAB, D), ((0, 256),), -0.2, 0.2)), 0.05, 2.0)
    return {"acts": acts, "logit_grad": logit_grad, "token_ids": token_ids, "table": table, "moment_one": moment_one, "moment_two": moment_two}


corr_first = 1.0 - 0.9 ** 10
corr_second = 1.0 - 0.95 ** 10

def reference(acts, logit_grad, token_ids, table, moment_one, moment_two):
    hidden = acts[1].reshape(-1, D).astype(jnp.float32)
    cotangent = acts[0].reshape(-1, D).astype(jnp.float32)
    logits = logit_grad.reshape(-1, VOCAB).astype(jnp.float32)
    head_grad = jnp.dot(logits.T, hidden, precision=lax.Precision.HIGHEST)
    id_rows = token_ids.reshape(-1)
    safe_rows = jnp.where(id_rows < VOCAB, id_rows, VOCAB).astype(jnp.int32)
    embed_grad = jax.ops.segment_sum(cotangent, safe_rows, num_segments=VOCAB + 1)[:VOCAB]
    gradient = head_grad + embed_grad
    new_one = 0.9 * moment_one + 0.1 * gradient
    new_two = 0.95 * moment_two + 0.05 * gradient * gradient
    update = new_one / corr_first / (jnp.sqrt(new_two / corr_second) + 1e-08)
    new_table = table - 0.01 * (update + 0.1 * table)
    return (new_table, new_one, new_two)
```

```python
import functools

import jax
import jax.numpy as jnp
from jax import lax
from jax.experimental import pallas as pl
from jax.experimental.pallas import tpu as pltpu
from jax.sharding import PartitionSpec as P

corr_first = 1.0 - 0.9**10
corr_second = 1.0 - 0.95**10

AXES = ("section", "shard", "rep")
RING = 4
CAP_CHUNK = 16
CAP_ROUTE = 16
SUBS = ((0, 9),)
LANE = 128


def index_of(section, y, x, z_hi, rep):
    return (section * 64 + (y * RING + x) * RING + z_hi) * 2 + rep


def pairs(move):
    out = []
    for section in range(2):
        for y in range(RING):
            for x in range(RING):
                for z_hi in range(RING):
                    for rep in range(2):
                        out.append((index_of(section, y, x, z_hi, rep), index_of(*move(section, y, x, z_hi, rep))))
    return out


def quad_pairs(a, b):
    return pairs(lambda s, y, x, z, r: (s ^ a, y, x, z, r ^ b))


def depth_pairs(step):
    return pairs(lambda s, y, x, z, r: (s, y, x, (z + step) % RING, r))


def second_pairs(step):
    return pairs(lambda s, y, x, z, r: (s, (y + step * r) % RING, (x + step * (1 - r)) % RING, z, r))


def last_pairs(step):
    return pairs(lambda s, y, x, z, r: (s, (y + step * (1 - r)) % RING, (x + step * r) % RING, z, r))


def send(array, table):
    return lax.ppermute(array, AXES, table)


def pick(mask, first, second):
    return jnp.where(mask, first, second)


def roll_to(array, shift, axis):
    size = array.shape[axis]
    head = lax.slice_in_dim(array, 0, size - 1, axis=axis)
    return lax.dynamic_slice_in_dim(jnp.concatenate([array, head], axis), shift, size, axis)


def slots_of(mask, cap):
    size = mask.shape[-1]
    upto = lax.broadcasted_iota(jnp.int32, (size, size), 0) <= lax.broadcasted_iota(jnp.int32, (size, size), 1)
    counts = mask.astype(jnp.int32)
    rank = jnp.sum(counts[..., :, None] * upto.astype(jnp.int32), axis=-2) - 1
    places = lax.broadcasted_iota(jnp.int32, (cap, 1), 0)
    return jnp.logical_and(rank[..., None, :] == places, mask[..., None, :])


def adamw_kernel(where_ref, g_ref, t_ref, m_ref, v_ref, *rest):
    t_out, m_out, v_out = rest[-3:]
    g = g_ref[...]
    new_one = 0.9 * m_ref[...] + 0.1 * g
    new_two = 0.95 * v_ref[...] + 0.05 * g * g
    update = new_one / corr_first / (jnp.sqrt(new_two / corr_second) + 1e-08)
    t = t_ref[...]
    t_out[...] = t - 0.01 * (update + 0.1 * t)
    m_out[...] = new_one
    v_out[...] = new_two


def adamw_part(where, g, table, one, two, previous, step):
    rows, width = g.shape
    wide = pl.BlockSpec((rows, step), lambda i, where_ref: (0, where_ref[0] + i))
    specs = [pl.BlockSpec((rows, step), lambda i, where_ref: (0, i)), wide, wide, wide]
    args = [g, table, one, two]
    aliases = {}
    if previous is not None:
        specs += [pl.BlockSpec(memory_space=pl.ANY)] * 3
        args += list(previous)
        aliases = {5: 0, 6: 1, 7: 2}
    return pl.pallas_call(
        adamw_kernel,
        grid_spec=pltpu.PrefetchScalarGridSpec(
            num_scalar_prefetch=1, grid=(width // step,), in_specs=specs, out_specs=[wide] * 3
        ),
        out_shape=[jax.ShapeDtypeStruct(table.shape, jnp.float32)] * 3,
        input_output_aliases=aliases,
        cost_estimate=pl.CostEstimate(flops=16 * rows * width, bytes_accessed=28 * rows * width, transcendentals=rows * width),
        compiler_params=pltpu.CompilerParams(vmem_limit_bytes=16 * 1024 * 1024),
    )(where, *args)


def dot_rows(weights, rows):
    return lax.dot_general(weights, rows, (((0,), (0,)), ((), ())), preferred_element_type=jnp.float32)


def full_embedding(acts, own_ids, section, shard, quarter, voc, width):
    tokens = acts.shape[0]
    step = pairs(lambda s, y, x, z, r: (s, (y + (x + (z + 1) // RING) // RING) % RING, (x + (z + 1) // RING) % RING, (z + 1) % RING, r))
    rows = shard * voc + lax.broadcasted_iota(jnp.int32, (1, voc), 1)

    def body(i, state):
        current, total = state
        source = lax.rem(shard - i + 64, 64)
        ids = lax.dynamic_slice_in_dim(own_ids, source * tokens, tokens, 0)
        hot = jnp.logical_and(ids[:, None] == rows, section == 0).astype(jnp.bfloat16)
        return send(current, step), total + dot_rows(hot, current)

    total = lax.fori_loop(0, 64, body, (acts, jnp.zeros((voc, acts.shape[1]), jnp.float32)))[1]
    total = total + send(total, quad_pairs(0, 1))
    total = total + send(total, quad_pairs(1, 0))
    return lax.dynamic_slice_in_dim(total, quarter * width, width, 1)


def local(acts, logit_grad, token_ids, table, moment_one, moment_two):
    section = lax.axis_index("section")
    shard = lax.axis_index("shard")
    rep = lax.axis_index("rep")
    y, x, z_hi = shard // 16, lax.rem(shard // 4, 4), lax.rem(shard, 4)
    on_first = rep == 0
    second, last = pick(on_first, x, y), pick(on_first, y, x)
    quarter = 2 * section + rep

    own_acts = acts[0, 0]
    own_logits = logit_grad[0]
    own_ids = token_ids[0]
    tokens, model = own_acts.shape
    voc = own_logits.shape[1]
    width = model // 4
    part = voc // 4

    pieces = {}
    for a, b in ((1, 0), (1, 1), (0, 1), (0, 0)):
        block = lax.dynamic_slice_in_dim(own_acts, (2 * (section ^ a) + (rep ^ b)) * width, width, 1)
        pieces[a, b] = send(block, quad_pairs(a, b)) if (a, b) != (0, 0) else block

    def from_device(s, r):
        flip = rep != r
        same = jnp.where(flip, pieces[0, 1], pieces[0, 0])
        other = jnp.where(flip, pieces[1, 1], pieces[1, 0])
        return jnp.where(section == s, same, other)

    hidden = jnp.concatenate([from_device(1, 0), from_device(1, 1)], 0)
    cotangent = jnp.concatenate([from_device(0, 0), from_device(0, 1)], 0)

    other_ids = send(own_ids, quad_pairs(0, 1))
    other_logits = send(own_logits, quad_pairs(0, 1))

    ids = jnp.stack([pick(on_first, own_ids, other_ids), pick(on_first, other_ids, own_ids)])
    ids = ids.reshape(2, 64, tokens).transpose(1, 0, 2).reshape(64, 2 * tokens)
    hit = jnp.logical_and(ids >= 0, ids < voc * 64)
    chunk_hot = slots_of(hit, CAP_CHUNK)
    chunk_ids = jnp.sum(jnp.where(chunk_hot, ids[:, None, :] + 1, 0), -1) - 1
    column_ids = chunk_ids.reshape(16, 4 * CAP_CHUNK)
    column_shard = jnp.where(column_ids >= 0, column_ids // voc, -1)
    targets = lax.broadcasted_iota(jnp.int32, (1, 4, 1), 1)
    live = column_shard[:, None, :] >= 0
    to_x = jnp.logical_and(lax.rem(column_shard[:, None, :] // 4, 4) == targets, live)
    to_y = jnp.logical_and(column_shard[:, None, :] // 16 == targets, live)
    to_second = pick(on_first, to_x, to_y)
    route_hot = slots_of(to_second, CAP_ROUTE)
    route_ids = jnp.sum(jnp.where(route_hot, column_ids[:, None, None, :] + 1, 0), -1) - 1
    overflow = jnp.logical_or(
        jnp.max(jnp.sum(hit.astype(jnp.int32), -1)) > CAP_CHUNK,
        jnp.logical_or(
            jnp.max(jnp.sum(to_x.astype(jnp.int32), -1)) > CAP_ROUTE,
            jnp.max(jnp.sum(to_y.astype(jnp.int32), -1)) > CAP_ROUTE,
        ),
    )

    mine = lax.dynamic_index_in_dim(route_ids, second, 1, keepdims=False).reshape(4, 4, CAP_ROUTE)
    mine = pick(on_first, mine, mine.swapaxes(0, 1))
    mine = roll_to(mine, second, 1)
    mine = jnp.where(overflow, -1, mine)
    vocab = shard * voc + lax.broadcasted_iota(jnp.int32, (1, 1, 1, voc), 3)
    slot_weights = (mine[..., None] == vocab).astype(jnp.bfloat16)

    group = 4 * tokens
    first_logits = pick(on_first, own_logits, other_logits).reshape(4, 4, group, voc)
    other_half = pick(on_first, other_logits, own_logits).reshape(4, 4, group, voc)

    def weights_of(offset):
        index = lax.rem(last + offset, 4)

        def rows_of(array):
            return pick(
                on_first,
                lax.dynamic_index_in_dim(array, index, 0, keepdims=False),
                lax.dynamic_index_in_dim(array, index, 1, keepdims=False),
            )

        hot = lax.dynamic_index_in_dim(slot_weights, index, 0, keepdims=False)
        both = jnp.concatenate([rows_of(first_logits), rows_of(other_half)], 1)
        return jnp.concatenate([roll_to(both, second, 0), hot], 1).reshape(-1, voc)

    weights = [weights_of(offset) for offset in range(4)]

    own_hot = lax.dynamic_index_in_dim(chunk_hot, shard, 0, keepdims=False).astype(jnp.bfloat16)
    own_route = lax.dynamic_index_in_dim(route_hot, y * 4 + x, 0, keepdims=False)
    own_route = roll_to(own_route, second, 0).astype(jnp.bfloat16).reshape(4 * CAP_ROUTE, 4 * CAP_CHUNK)

    start_total = lax.cond(
        overflow,
        lambda: full_embedding(own_acts, own_ids, section, shard, quarter, voc, width),
        lambda: jnp.zeros((voc, width), jnp.float32),
    )

    results = None
    for block_from, blocks in SUBS:
        low, wide = block_from * LANE, blocks * LANE
        here = lax.slice_in_dim(hidden, low, low + wide, axis=1)
        there = lax.slice_in_dim(cotangent, low, low + wide, axis=1)
        kept = jnp.dot(own_hot, there, preferred_element_type=jnp.float32).astype(jnp.bfloat16)
        chunk = jnp.concatenate([here, kept], 0)

        up, down, far = (send(chunk, depth_pairs(step)) for step in (1, -1, 2))
        column = jnp.stack([chunk, down, far, up])
        column = roll_to(column, lax.rem(4 - z_hi, 4), 0)
        spoken = column[:, : 2 * tokens].reshape(4, 2, tokens, wide).transpose(1, 0, 2, 3).reshape(8 * tokens, wide)
        kept = column[:, 2 * tokens :].reshape(4 * CAP_CHUNK, wide)

        routed = jnp.dot(own_route, kept, preferred_element_type=jnp.float32).astype(jnp.bfloat16)
        outgoing = [jnp.concatenate([spoken, routed[k * CAP_ROUTE : (k + 1) * CAP_ROUTE]], 0) for k in range(4)]
        up = send(outgoing[1], second_pairs(1))
        down = send(outgoing[3], second_pairs(-1))
        far = send(outgoing[2], second_pairs(2))
        plane = jnp.concatenate([outgoing[0], down, far, up], 0)

        half = plane.shape[0] // 2
        lower, upper = plane[:half], plane[half:]
        before_lower = send(lower, last_pairs(1))
        after_upper = send(upper, last_pairs(-1))
        before_upper = send(upper, last_pairs(1))
        after_lower = send(lower, last_pairs(-1))
        far_lower = send(before_lower, last_pairs(1))
        far_upper = send(after_upper, last_pairs(-1))
        total = lax.slice_in_dim(start_total, low, low + wide, axis=1) + dot_rows(weights[0], plane)
        for offset, first, block in (
            (3, True, before_lower),
            (1, False, after_upper),
            (3, False, before_upper),
            (1, True, after_lower),
            (2, True, far_lower),
            (2, False, far_upper),
        ):
            chosen = weights[offset][:half] if first else weights[offset][half:]
            total = total + dot_rows(chosen, block)

        for a, b in ((0, 0), (0, 1), (1, 0), (1, 1)):
            block = lax.dynamic_slice_in_dim(total, (2 * (section ^ a) + (rep ^ b)) * part, part, 0)
            if (a, b) != (0, 0):
                block = send(block, quad_pairs(a, b))
            step = wide if wide == width else LANE
            place = (2 * (section ^ a) + (rep ^ b)) * (width // step) + low // step
            results = adamw_part(
                place.reshape(1).astype(jnp.int32), block, table, moment_one, moment_two, results, step
            )
    return tuple(results)


def solution(mesh):
    rows = P(("shard", "section", "rep"), None)
    return jax.shard_map(
        local,
        mesh=mesh,
        in_specs=(P("section", "rep", "shard", None), P("rep", None, "shard"), P("rep", None), rows, rows, rows),
        out_specs=(rows, rows, rows),
        check_vma=False,
    )
```

```python
import functools

import jax
import jax.numpy as jnp
from jax import lax
from jax.experimental import pallas as pl
from jax.experimental.pallas import tpu as pltpu
from jax.sharding import PartitionSpec as P

corr_first = 1.0 - 0.9**10
corr_second = 1.0 - 0.95**10

AXES = ("section", "shard", "rep")
RING = 4
CAP_CHUNK = 16
CAP_ROUTE = 16
SMALL = pl.CostEstimate(flops=1024, bytes_accessed=1024, transcendentals=0)


def index_of(section, y, x, z_hi, rep):
    return (section * 64 + (y * RING + x) * RING + z_hi) * 2 + rep


def pairs(move):
    out = []
    for section in range(2):
        for y in range(RING):
            for x in range(RING):
                for z_hi in range(RING):
                    for rep in range(2):
                        out.append((index_of(section, y, x, z_hi, rep), index_of(*move(section, y, x, z_hi, rep))))
    return out


def quad_pairs(a, b):
    return pairs(lambda s, y, x, z, r: (s ^ a, y, x, z, r ^ b))


def depth_pairs(step):
    return pairs(lambda s, y, x, z, r: (s, y, x, (z + step) % RING, r))


def second_pairs(step):
    return pairs(lambda s, y, x, z, r: (s, (y + step * r) % RING, (x + step * (1 - r)) % RING, z, r))


def last_pairs(step):
    return pairs(lambda s, y, x, z, r: (s, (y + step * (1 - r)) % RING, (x + step * r) % RING, z, r))


def send(array, table):
    return lax.ppermute(array, AXES, table)


def pick(mask, first, second):
    return jnp.where(mask, first, second)


def roll_to(array, shift, axis):
    size = array.shape[axis]
    head = lax.slice_in_dim(array, 0, size - 1, axis=axis)
    return lax.dynamic_slice_in_dim(jnp.concatenate([array, head], axis), shift, size, axis)


def slots_of(mask, cap):
    size = mask.shape[-1]
    upto = lax.broadcasted_iota(jnp.int32, (size, size), 0) <= lax.broadcasted_iota(jnp.int32, (size, size), 1)
    counts = mask.astype(jnp.int32)
    rank = jnp.sum(counts[..., :, None] * upto.astype(jnp.int32), axis=-2) - 1
    places = lax.broadcasted_iota(jnp.int32, (cap, 1), 0)
    return jnp.logical_and(rank[..., None, :] == places, mask[..., None, :])


def in_hbm(array):
    return pltpu.with_memory_space_constraint(array, pltpu.HBM)


def adamw_kernel(where_ref, g_ref, t_ref, m_ref, v_ref, *refs):
    t_out, m_out, v_out = refs[-3:]
    g = g_ref[...]
    new_one = 0.9 * m_ref[...] + 0.1 * g
    new_two = 0.95 * v_ref[...] + 0.05 * g * g
    update = new_one / corr_first / (jnp.sqrt(new_two / corr_second) + 1e-08)
    t = t_ref[...]
    t_out[...] = t - 0.01 * (update + 0.1 * t)
    m_out[...] = new_one
    v_out[...] = new_two


def adamw_part(where, g, state, previous, *order):
    rows, width = g.shape
    inner = pl.BlockSpec((rows, width), lambda i, where_ref: (0, where_ref[1]))
    wide = pl.BlockSpec((rows, width), lambda i, where_ref: (0, where_ref[0]))
    anywhere = pl.BlockSpec(memory_space=pl.ANY)
    specs = [pl.BlockSpec((rows, width), lambda i, where_ref: (0, 0))] + [inner] * 3 + [anywhere] * len(order)
    args = [g, *state, *order]
    aliases = {}
    if previous is not None:
        aliases = {1 + len(args) + i: i for i in range(3)}
        specs += [anywhere] * 3
        args += list(previous)
    return pl.pallas_call(
        adamw_kernel,
        grid_spec=pltpu.PrefetchScalarGridSpec(num_scalar_prefetch=1, grid=(1,), in_specs=specs, out_specs=[wide] * 3),
        out_shape=[jax.ShapeDtypeStruct((rows, 4 * width), jnp.float32)] * 3,
        input_output_aliases=aliases,
        cost_estimate=SMALL,
        compiler_params=pltpu.CompilerParams(vmem_limit_bytes=8 * 1024 * 1024),
    )(where, *args)


def fetch_kernel(where_ref, *refs):
    sources, outs, sems = refs[:3], refs[4:7], refs[7]
    width = outs[0].shape[1]
    columns = pl.ds(pl.multiple_of(where_ref[0] * width, 128), width)
    copies = [pltpu.make_async_copy(a.at[:, columns], b, sems.at[k]) for k, (a, b) in enumerate(zip(sources, outs))]
    for copy in copies:
        copy.start()
    for copy in copies:
        copy.wait()


def fetch(where, arrays, order):
    anywhere = pl.BlockSpec(memory_space=pl.ANY)
    rows, width = arrays[0].shape
    return pl.pallas_call(
        fetch_kernel,
        in_specs=[pl.BlockSpec(memory_space=pltpu.SMEM)] + [anywhere] * 4,
        out_specs=[pl.BlockSpec(memory_space=pltpu.VMEM)] * 3,
        out_shape=[pltpu.VMEM((rows, width // 2), array.dtype) for array in arrays],
        scratch_shapes=[pltpu.SemaphoreType.DMA((3,))],
        cost_estimate=SMALL,
        compiler_params=pltpu.CompilerParams(vmem_limit_bytes=4 * 1024 * 1024),
    )(where, *map(in_hbm, arrays), order)


def cut_kernel(where_ref, acts, *outs):
    width = outs[0].shape[1]
    for k, out in enumerate(outs):
        out[...] = acts[:, pl.ds(pl.multiple_of(where_ref[k] * width, 128), width)]


def cut_quarters(where, acts):
    rows, model = acts.shape
    vmem = pl.BlockSpec(memory_space=pltpu.VMEM)
    return pl.pallas_call(
        cut_kernel,
        in_specs=[pl.BlockSpec(memory_space=pltpu.SMEM), vmem],
        out_specs=[vmem] * 4,
        out_shape=[jax.ShapeDtypeStruct((rows, model // 4), acts.dtype)] * 4,
        cost_estimate=SMALL,
        compiler_params=pltpu.CompilerParams(vmem_limit_bytes=4 * 1024 * 1024),
    )(where, in_hbm(acts))


def spread_kernel(where_ref, route, *refs):
    pieces, outs = refs[:4], refs[4:]
    spoken = pieces[0].shape[0] - CAP_CHUNK
    routed = jnp.dot(route[:, :CAP_CHUNK], pieces[0][spoken:, :], preferred_element_type=jnp.float32)
    for k in range(1, 4):
        columns = slice(k * CAP_CHUNK, (k + 1) * CAP_CHUNK)
        routed += jnp.dot(route[:, columns], pieces[k][spoken:, :], preferred_element_type=jnp.float32)
    routed = routed.astype(jnp.bfloat16)
    for k in range(4):
        low = pl.multiple_of(((where_ref[0] + k) & 3) * spoken, 16)
        for out in outs:
            out[pl.ds(low, spoken), :] = pieces[k][:spoken, :]
        outs[k][4 * spoken :, :] = routed[k * CAP_ROUTE : (k + 1) * CAP_ROUTE]


def spread(z_hi, route, pieces):
    tall, width = pieces[0].shape
    rows = 4 * (tall - CAP_CHUNK) + CAP_ROUTE
    return pl.pallas_call(
        spread_kernel,
        in_specs=[pl.BlockSpec(memory_space=pltpu.SMEM)] + [pl.BlockSpec(memory_space=pltpu.VMEM)] * 5,
        out_specs=[pl.BlockSpec(memory_space=pltpu.VMEM)] * 4,
        out_shape=[jax.ShapeDtypeStruct((rows, width), jnp.bfloat16)] * 4,
        cost_estimate=SMALL,
        compiler_params=pltpu.CompilerParams(vmem_limit_bytes=4 * 1024 * 1024),
    )(z_hi.reshape(1), route, *pieces)


def join_kernel(first, second, *refs):
    out = refs[-1]
    rows = first.shape[0]
    out[:rows, :] = first[...]
    out[rows:, :] = second[...]


def join(first, second, *order):
    rows, width = first.shape
    vmem = pl.BlockSpec(memory_space=pltpu.VMEM)
    return pl.pallas_call(
        join_kernel,
        in_specs=[vmem, vmem] + [pl.BlockSpec(memory_space=pl.ANY)] * len(order),
        out_specs=vmem,
        out_shape=jax.ShapeDtypeStruct((2 * rows, width), first.dtype),
        cost_estimate=SMALL,
        compiler_params=pltpu.CompilerParams(vmem_limit_bytes=4 * 1024 * 1024),
    )(first, second, *order)


def prepare_kernel(group, where_ref, ids_ref, own_hbm, other_hbm, pass_in, *outs):
    weights, flags, largest = outs[:8], outs[8], outs[9]
    own, other, sems = outs[11:]
    copies = [pltpu.make_async_copy(a, b, sems.at[k]) for k, (a, b) in enumerate(zip((own_hbm, other_hbm), (own, other)))]
    for copy in copies:
        copy.start()
    voc = own.shape[1]
    tokens = group // 4
    rows = 2 * group + CAP_ROUTE
    ids = ids_ref[...]
    spots = ids.shape[1]
    hit = ids < voc * 64
    home = jnp.where(hit, ids // voc, -1)
    place = lax.broadcasted_iota(jnp.int32, ids.shape, 1) // (2 * tokens)
    most = jnp.int32(0)
    for k in range(4):
        in_chunk = jnp.sum(jnp.where(jnp.logical_and(hit, place == k), 1, 0), 1, keepdims=True)
        to_x = jnp.sum(jnp.where(jnp.logical_and(hit, (home >> 2) & 3 == k), 1, 0), 1, keepdims=True)
        to_y = jnp.sum(jnp.where(jnp.logical_and(hit, home >> 4 == k), 1, 0), 1, keepdims=True)
        excess = jnp.maximum(in_chunk - CAP_CHUNK, jnp.maximum(to_x, to_y) - CAP_ROUTE)
        most = jnp.maximum(most, jnp.max(excess))
    flags[0] = most
    mine = jnp.where(where_ref[34] == 0, (home >> 2) & 3, home >> 4) == where_ref[32]
    mine = jnp.logical_and(hit, mine)
    upto = lax.broadcasted_iota(jnp.int32, (spots, spots), 0) <= lax.broadcasted_iota(jnp.int32, (spots, spots), 1)
    rank = jnp.dot(
        jnp.where(mine, 1.0, 0.0).astype(jnp.bfloat16),
        jnp.where(upto, 1.0, 0.0).astype(jnp.bfloat16),
        preferred_element_type=jnp.float32,
    ).astype(jnp.int32)
    rank = jnp.where(jnp.logical_and(mine, most <= 0), rank, 0)
    number = lax.broadcasted_iota(jnp.int32, (CAP_ROUTE, spots), 0) + 1
    columns = lax.broadcasted_iota(jnp.int32, (CAP_ROUTE, voc), 1) + where_ref[33]
    flags[1] = jnp.sum(jnp.where(jnp.logical_and(mine, home * voc == where_ref[33]), 1, 0))

    slots = []
    for c in range(16):
        chosen = rank[c : c + 1, :] == number
        slots.append(jnp.sum(jnp.where(chosen, ids[c : c + 1, :] + 1, 0), 1, keepdims=True) - 1)
    slots = jnp.concatenate(slots, 0)
    for copy in copies:
        copy.wait()
    top = jnp.float32(0)
    for n in range(16):
        out, low = weights[n // 2], n % 2 * rows
        at = pl.multiple_of(where_ref[n] * group, 16)
        first, second = own[pl.ds(at, group), :], other[pl.ds(at, group), :]
        for z in range(4):
            both = [array[z * tokens : (z + 1) * tokens, :] for array in (first, second)]
            out[low + 2 * z * tokens : low + 2 * (z + 1) * tokens, :] = jnp.concatenate(both, 0)
        top = jnp.maximum(top, jnp.max(jnp.abs(first.astype(jnp.float32))))
        top = jnp.maximum(top, jnp.max(jnp.abs(second.astype(jnp.float32))))
        picked = jnp.full((CAP_ROUTE, 1), -1, jnp.int32)
        for c in range(16):
            picked = jnp.where(where_ref[16 + n] == c, slots[c * CAP_ROUTE : (c + 1) * CAP_ROUTE, :], picked)
        out[low + 2 * group : low + rows, :] = jnp.where(picked == columns, 1.0, 0.0).astype(jnp.bfloat16)
    largest[0] = top


def prepare(where, ids, own, other, passing, group):
    voc = own.shape[1]
    rows = 2 * (2 * group + CAP_ROUTE)
    vmem, smem = pl.BlockSpec(memory_space=pltpu.VMEM), pl.BlockSpec(memory_space=pltpu.SMEM)
    anywhere = pl.BlockSpec(memory_space=pl.ANY)
    return pl.pallas_call(
        functools.partial(prepare_kernel, group),
        in_specs=[smem, vmem] + [anywhere] * 3,
        out_specs=[vmem] * 8 + [smem, smem, anywhere],
        out_shape=[pltpu.VMEM((rows, voc), jnp.bfloat16)] * 8
        + [jax.ShapeDtypeStruct((2,), jnp.int32), jax.ShapeDtypeStruct((1,), jnp.float32)]
        + [jax.ShapeDtypeStruct(passing.shape, passing.dtype)],
        input_output_aliases={4: 10},
        scratch_shapes=[pltpu.VMEM(own.shape, own.dtype)] * 2 + [pltpu.SemaphoreType.DMA((2,))],
        cost_estimate=SMALL,
        compiler_params=pltpu.CompilerParams(vmem_limit_bytes=8 * 1024 * 1024),
    )(where, ids, in_hbm(own), other, passing)


def add_products(total, products):
    for weights, rows in products:
        total = total + dot_rows(weights, rows)
    return total


def dot_rows(weights, rows):
    return lax.dot_general(weights, rows, (((0,), (0,)), ((), ())), preferred_element_type=jnp.float32)


def full_embedding(acts, own_ids, section, shard, quarter, voc, width):
    tokens = acts.shape[0]
    step = pairs(lambda s, y, x, z, r: (s, (y + (x + (z + 1) // RING) // RING) % RING, (x + (z + 1) // RING) % RING, (z + 1) % RING, r))
    rows = shard * voc + lax.broadcasted_iota(jnp.int32, (1, voc), 1)

    def body(i, state):
        current, total = state
        source = lax.rem(shard - i + 64, 64)
        ids = lax.dynamic_slice_in_dim(own_ids, source * tokens, tokens, 0)
        hot = jnp.logical_and(ids[:, None] == rows, section == 0).astype(jnp.bfloat16)
        return send(current, step), total + dot_rows(hot, current)

    total = lax.fori_loop(0, 64, body, (acts, jnp.zeros((voc, acts.shape[1]), jnp.float32)))[1]
    total = total + send(total, quad_pairs(0, 1))
    total = total + send(total, quad_pairs(1, 0))
    return lax.dynamic_slice_in_dim(total, quarter * width, width, 1)


def local(acts, logit_grad, token_ids, table, moment_one, moment_two):
    section = lax.axis_index("section")
    shard = lax.axis_index("shard")
    rep = lax.axis_index("rep")
    y, x, z_hi = shard >> 4, (shard >> 2) & 3, shard & 3
    on_first = rep == 0
    second, last = pick(on_first, x, y), pick(on_first, y, x)
    quarter = 2 * section + rep

    own_acts = acts[0, 0]
    own_logits = logit_grad[0]
    tokens, model = own_acts.shape
    voc = own_logits.shape[1]
    width = model // 4
    part = voc // 4

    pieces = {}
    flips = ((1, 0), (1, 1), (0, 1), (0, 0))
    takers = jnp.stack([2 * (section ^ a) + (rep ^ b) for a, b in flips]).astype(jnp.int32)
    for (a, b), block in zip(flips, cut_quarters(takers, own_acts)):
        pieces[a, b] = send(block, quad_pairs(a, b)) if (a, b) != (0, 0) else block

    hidden = jnp.concatenate([jnp.where(section == 1, pieces[0, b], pieces[1, b]) for b in (0, 1)], 0)
    cotangent = jnp.concatenate([jnp.where(section == 0, pieces[0, b], pieces[1, b]) for b in (0, 1)], 0)

    other_ids = send(token_ids, quad_pairs(0, 1))
    other_logits = send(own_logits, quad_pairs(0, 1))

    ids = jnp.concatenate([token_ids, other_ids], 0)
    own_chunk = lax.dynamic_slice_in_dim(ids, shard * tokens, tokens, 1).reshape(2 * tokens)
    own_hot = slots_of(own_chunk < voc * 64, CAP_CHUNK).astype(jnp.bfloat16)

    kept = jnp.dot(own_hot, cotangent, preferred_element_type=jnp.float32).astype(jnp.bfloat16)
    chunk = jnp.concatenate([hidden, kept], 0)

    down, far, up = (send(chunk, depth_pairs(step)) for step in (-1, 2, 1))

    targets = lax.broadcasted_iota(jnp.int32, (1, 4, 1), 1)

    def routes(shards):
        live = shards[:, None, :] >= 0
        to_x = jnp.logical_and((shards[:, None, :] >> 2) & 3 == targets, live)
        to_y = jnp.logical_and(shards[:, None, :] >> 4 == targets, live)
        return to_x, to_y

    def kept_ids(ids):
        hit = ids < voc * 64
        hot = slots_of(hit, CAP_CHUNK)
        return hit, (jnp.sum(jnp.where(hot, ids[:, None, :] + 1, 0), -1) - 1).reshape(-1, 4 * CAP_CHUNK)

    def shards_of(column_ids):
        return jnp.where(column_ids >= 0, column_ids // voc, -1)

    own_column = lax.dynamic_slice_in_dim(ids, (shard >> 2) * 4 * tokens, 4 * tokens, 1)
    own_column = own_column.reshape(2, 4, tokens).transpose(1, 0, 2).reshape(4, 2 * tokens)
    own_route = slots_of(pick(on_first, *routes(shards_of(kept_ids(own_column)[1]))), CAP_ROUTE)[0]
    own_route = roll_to(own_route, second, 0).reshape(4 * CAP_ROUTE, 4, CAP_CHUNK)
    own_route = roll_to(own_route, z_hi, 1).astype(jnp.bfloat16).reshape(4 * CAP_ROUTE, 4 * CAP_CHUNK)

    outgoing = list(spread(z_hi, own_route, [chunk, down, far, up]))

    columns = ids.reshape(2, 16, 4, tokens).transpose(1, 2, 0, 3).reshape(16, 8 * tokens)
    turning = [(second + k) & 3 for k in range(4)]
    order = [((last + offset) & 3, turn) for offset in range(4) for turn in turning]
    places = [pick(on_first, 4 * fixed + turn, 4 * turn + fixed) for fixed, turn in order]
    where = jnp.stack([*places, *places, second, shard * voc, rep]).astype(jnp.int32)
    *weights, flags, largest, outgoing[2] = prepare(
        where, columns, own_logits, other_logits, outgoing[2], 4 * tokens
    )
    weights = [weights[2 * k : 2 * k + 2] for k in range(4)]
    plane = [outgoing[0], *(send(outgoing[k], second_pairs(step)) for k, step in ((3, -1), (2, 2), (1, 1)))]
    overflow, touched = flags[0] > 0, flags[1] > 0

    start_total = lax.cond(
        overflow,
        lambda: full_embedding(own_acts, token_ids[0], section, shard, quarter, voc, width),
        lambda: jnp.zeros((voc, width), jnp.float32),
    )

    lower, upper = join(plane[0], plane[1], largest, *plane[2:]), join(plane[2], plane[3], largest, plane[1])
    before, behind = [send(lower, last_pairs(1))], [send(upper, last_pairs(-1))]
    total = add_products(start_total, [(weights[0][0], lower), (weights[0][1], upper)])
    before.append(send(upper, last_pairs(1)))
    behind.append(send(lower, last_pairs(-1)))
    far = send(before[0], last_pairs(1)), send(behind[0], last_pairs(-1))
    total = add_products(total, [(weights[3][0], before[0]), (weights[1][1], behind[0])])
    total = add_products(total, [(weights[3][1], before[1]), (weights[1][0], behind[1])])
    total = add_products(total, [(weights[2][0], far[0]), (weights[2][1], far[1])])

    bound = 6.0 * 2 * 64 * tokens * (largest[0] + touched.astype(jnp.float32))
    bound = jnp.where(jnp.logical_or(overflow, bound <= 0), 6.0 * 2 * 64 * tokens * 2, bound)
    scale = 32768.0 / bound

    sent = {}
    for a, b in ((1, 0), (1, 1), (0, 1), (0, 0)):
        row = (2 * (section ^ a) + (rep ^ b)) * part
        block = lax.dynamic_slice_in_dim(total, row, part, 0)
        if a:
            block = (block * scale).astype(jnp.float16)
        sent[a, b] = send(block, quad_pairs(a, b)) if (a, b) != (0, 0) else block
    state = (table, moment_one, moment_two)
    across = fetch((section ^ 1).reshape(1).astype(jnp.int32), state, sent[0, 0])
    results = None
    for a, b in ((0, 0), (0, 1), (1, 0), (1, 1)):
        place = 2 * (section ^ a) + (rep ^ b)
        if a:
            block = sent[a, b].astype(jnp.float32) * (1.0 / scale)
            results = adamw_part(jnp.stack([place, rep ^ b]).astype(jnp.int32), block, across, results)
        else:
            place = jnp.stack([place, place]).astype(jnp.int32)
            results = adamw_part(place, sent[a, b], list(map(in_hbm, state)), results, across[0])
    return tuple(results)


def solution(mesh):
    rows = P(("shard", "section", "rep"), None)
    return jax.shard_map(
        local,
        mesh=mesh,
        in_specs=(P("section", "rep", "shard", None), P("rep", None, "shard"), P("rep", None), rows, rows, rows),
        out_specs=(rows, rows, rows),
        check_vma=False,
    )
```

```python
import functools

import jax
import jax.numpy as jnp
from jax import lax
from jax.experimental import pallas as pl
from jax.experimental.pallas import tpu as pltpu
from jax.sharding import PartitionSpec as P

corr_first = 1.0 - 0.9**10
corr_second = 1.0 - 0.95**10

AXES = ("section", "shard", "rep")
RING = 4
VOC_SHARD = 384
CAP_CHUNK = 16
CAP_ROUTE = 32
PARTS = (640, 512)
HALF = 640
SMALL = pl.CostEstimate(flops=1024, bytes_accessed=1024, transcendentals=0)


def index_of(section, y, x, z_hi, rep):
    return (section * 64 + (y * RING + x) * RING + z_hi) * 2 + rep


def pairs(move):
    out = []
    for section in range(2):
        for y in range(RING):
            for x in range(RING):
                for z_hi in range(RING):
                    for rep in range(2):
                        out.append((index_of(section, y, x, z_hi, rep), index_of(*move(section, y, x, z_hi, rep))))
    return out


def quad_pairs(a, b):
    return pairs(lambda s, y, x, z, r: (s ^ a, y, x, z, r ^ b))


def depth_pairs(step):
    return pairs(lambda s, y, x, z, r: (s, y, x, (z + step) % RING, r))


def second_pairs(step):
    return pairs(lambda s, y, x, z, r: (s, (y + step * r) % RING, (x + step * (1 - r)) % RING, z, r))


def last_pairs(step):
    return pairs(lambda s, y, x, z, r: (s, (y + step * (1 - r)) % RING, (x + step * r) % RING, z, r))


def pair_pairs(a, b):
    return pairs(lambda s, y, x, z, r: (s ^ a, y ^ r, x ^ (1 - r), z, r ^ b))


def send(array, table):
    return lax.ppermute(array, AXES, table)


def pick(mask, first, second):
    return jnp.where(mask, first, second)


def in_hbm(array):
    return pltpu.with_memory_space_constraint(array, pltpu.HBM)


def adamw_kernel(where_ref, held_ref, *refs):
    parts = len(PARTS)
    firsts, seconds = refs[:parts], refs[parts : 2 * parts]
    t_ref, m_ref, v_ref = refs[2 * parts : 2 * parts + 3]
    t_out, m_out, v_out, held_out = refs[-4:]
    held_out[...] = jnp.full(held_out.shape, held_ref[0], jnp.float32)
    low = 0
    for first, second in zip(firsts, seconds):
        at = (slice(None), slice(low, low + first.shape[1]))
        low += first.shape[1]
        g = jnp.where(pl.program_id(0) == 0, first[...], second[...])
        new_one = 0.9 * m_ref[at] + 0.1 * g
        new_two = 0.95 * v_ref[at] + 0.05 * g * g
        update = new_one / corr_first / (jnp.sqrt(new_two / corr_second) + 1e-08)
        t = t_ref[at]
        t_out[at] = t - 0.01 * (update + 0.1 * t)
        m_out[at] = new_one
        v_out[at] = new_two


def adamw_pair(where, held, first, second, state, previous, *order):
    rows, width = first[0].shape[0], sum(PARTS)
    inner = pl.BlockSpec((rows, width), lambda i, where_ref: (0, where_ref[2 + i]))
    wide = pl.BlockSpec((rows, width), lambda i, where_ref: (0, where_ref[i]))
    small = pl.BlockSpec((8, 128), lambda i, where_ref: (0, 0))
    anywhere = pl.BlockSpec(memory_space=pl.ANY)
    blocks = [*first, *second]
    specs = [pl.BlockSpec(memory_space=pltpu.SMEM)]
    specs += [pl.BlockSpec(block.shape, lambda i, where_ref: (0, 0)) for block in blocks]
    specs += [inner] * 3 + [anywhere] * len(order)
    args = [held, *blocks, *state, *order]
    aliases = {}
    if previous is not None:
        aliases = {1 + len(args) + i: i for i in range(3)}
        specs += [anywhere] * 3
        args += list(previous)
    return pl.pallas_call(
        adamw_kernel,
        grid_spec=pltpu.PrefetchScalarGridSpec(
            num_scalar_prefetch=1, grid=(2,), in_specs=specs, out_specs=[wide] * 3 + [small]
        ),
        out_shape=[jax.ShapeDtypeStruct((rows, 4 * width), jnp.float32)] * 3
        + [jax.ShapeDtypeStruct((8, 128), jnp.float32)],
        input_output_aliases=aliases,
        cost_estimate=SMALL,
        compiler_params=pltpu.CompilerParams(vmem_limit_bytes=10 * 1024 * 1024),
    )(where, *args)


def fetch_kernel(where_ref, *refs):
    sources, outs, sems = refs[:3], refs[4:7], refs[7]
    width = outs[0].shape[1]
    columns = pl.ds(pl.multiple_of(where_ref[0] * width, 128), width)
    copies = [pltpu.make_async_copy(a.at[:, columns], b, sems.at[k]) for k, (a, b) in enumerate(zip(sources, outs))]
    for copy in copies:
        copy.start()
    for copy in copies:
        copy.wait()


def fetch(where, arrays, order):
    anywhere = pl.BlockSpec(memory_space=pl.ANY)
    rows, width = arrays[0].shape
    return pl.pallas_call(
        fetch_kernel,
        in_specs=[pl.BlockSpec(memory_space=pltpu.SMEM)] + [anywhere] * 4,
        out_specs=[pl.BlockSpec(memory_space=pltpu.VMEM)] * 3,
        out_shape=[pltpu.VMEM((rows, width // 2), array.dtype) for array in arrays],
        scratch_shapes=[pltpu.SemaphoreType.DMA((3,))],
        cost_estimate=SMALL,
        compiler_params=pltpu.CompilerParams(vmem_limit_bytes=4 * 1024 * 1024),
    )(where, *map(in_hbm, arrays), order)


def cut_kernel(where_ref, ids, acts, *outs):
    width = outs[0].shape[1]
    for k, out in enumerate(outs[:4]):
        out[...] = acts[:, pl.ds(pl.multiple_of(where_ref[k] * width, 128), width)]
    outs[4][...] = ids[...]


def cut_quarters(where, ids, acts):
    rows, model = acts.shape
    vmem = pl.BlockSpec(memory_space=pltpu.VMEM)
    return pl.pallas_call(
        cut_kernel,
        in_specs=[pl.BlockSpec(memory_space=pltpu.SMEM)] + [vmem] * 2,
        out_specs=[vmem] * 5,
        out_shape=[pltpu.VMEM((rows, model // 4), acts.dtype)] * 4 + [pltpu.VMEM(ids.shape, ids.dtype)],
        cost_estimate=SMALL,
        compiler_params=pltpu.CompilerParams(vmem_limit_bytes=4 * 1024 * 1024),
    )(where, ids, in_hbm(acts))


def by_column(own_ids, other_ids, spots):
    sides = []
    for ids in (own_ids, other_ids):
        sides.append(jnp.concatenate([ids[:, c * spots : (c + 1) * spots] for c in range(16)], 0))
    return jnp.concatenate(sides, 1)


def spots_of(size, dim):
    at = lax.broadcasted_iota(jnp.int32, (size, size), dim)
    side, at = jnp.where(at < size // 2, 0, 1), jnp.where(at < size // 2, at, at - size // 2)
    tokens = size // 8
    z = jnp.where(at < tokens, 0, jnp.where(at < 2 * tokens, 1, jnp.where(at < 3 * tokens, 2, 3)))
    return z, at - z * tokens + side * tokens


def count(flags, upto):
    as_number = lambda mask: jnp.where(mask, 1.0, 0.0).astype(jnp.bfloat16)
    return jnp.dot(as_number(flags), as_number(upto), preferred_element_type=jnp.float32).astype(jnp.int32)


def chunk_kernel(where_ref, own_ids, other_ids, *refs):
    pieces, chunk, route = refs[:4], refs[4], refs[5]
    section, column, z_hi, second, rep = (where_ref[k] for k in range(5))
    tokens, width = pieces[0].shape
    here, there = (pieces[3], pieces[2]), (pieces[0], pieces[1])
    hidden = [jnp.where(section == 1, here[b][...], there[b][...]) for b in (0, 1)]
    cotangent = [jnp.where(section == 0, here[b][...], there[b][...]) for b in (0, 1)]
    chunk[: 2 * tokens, :] = jnp.concatenate(hidden, 0)

    ids = by_column(own_ids, other_ids, 4 * tokens)
    size = ids.shape[1]
    rows = lax.broadcasted_iota(jnp.int32, ids.shape, 0)
    ids = jnp.sum(jnp.where(rows == column, ids, 0), 0, keepdims=True)
    hit = ids < VOC_SHARD * 64
    home = jnp.where(hit, ids // VOC_SHARD, 0)
    pair = jnp.where(rep == 0, (home >> 3) & 1, home >> 5)
    z_from, t_from = spots_of(size, 0)
    z_to, t_to = spots_of(size, 1)
    in_chunk = jnp.logical_and(z_from == z_to, t_from <= t_to)
    in_column = jnp.logical_or(z_from < z_to, in_chunk)
    eight = lambda row: jnp.broadcast_to(row, (8, size))
    slot = count(eight(hit), in_chunk)[:1]
    as_number = lambda mask: jnp.where(mask, 1.0, 0.0).astype(jnp.bfloat16)

    number = lax.broadcasted_iota(jnp.int32, (CAP_CHUNK, size), 0) + 1
    mine = jnp.logical_and(hit, z_to[:1] == z_hi)
    chosen = as_number(jnp.logical_and(slot == number, mine))
    token = lax.broadcasted_iota(jnp.int32, (size, 2 * tokens), 1)
    token = as_number(token == t_from[:, : 2 * tokens])
    chosen = jnp.dot(chosen, token, preferred_element_type=jnp.float32).astype(jnp.bfloat16)
    both = jnp.concatenate(cotangent, 0)
    chunk[2 * tokens :, :] = jnp.dot(chosen, both, preferred_element_type=jnp.float32).astype(jnp.bfloat16)

    kept = jnp.logical_and(hit, slot <= CAP_CHUNK)
    candidate = ((z_to[:1] - z_hi) & 3) * CAP_CHUNK + slot - 1
    same = lax.broadcasted_iota(jnp.int32, (size, size), 0) == lax.broadcasted_iota(jnp.int32, (size, size), 1)
    candidate = jnp.sum(jnp.where(same, jnp.where(kept, candidate, -1), 0), 1, keepdims=True)
    places = as_number(candidate == lax.broadcasted_iota(jnp.int32, (size, 4 * CAP_CHUNK), 1))
    number = lax.broadcasted_iota(jnp.int32, (CAP_ROUTE, size), 0) + 1
    for d in range(4):
        wanted = jnp.logical_and(kept, pair == ((second + d) & 3) >> 1)
        rank = count(eight(wanted), in_column)[:1]
        going = as_number(jnp.logical_and(rank == number, wanted))
        route[d * CAP_ROUTE : (d + 1) * CAP_ROUTE, :] = jnp.dot(
            going, places, preferred_element_type=jnp.float32
        ).astype(jnp.bfloat16)


def build_chunk(where, own_ids, other_ids, pieces):
    tokens, width = pieces[0].shape
    vmem = pl.BlockSpec(memory_space=pltpu.VMEM)
    return pl.pallas_call(
        chunk_kernel,
        in_specs=[pl.BlockSpec(memory_space=pltpu.SMEM)] + [vmem] * 6,
        out_specs=[vmem] * 2,
        out_shape=[
            jax.ShapeDtypeStruct((2 * tokens + CAP_CHUNK, width), jnp.bfloat16),
            jax.ShapeDtypeStruct((4 * CAP_ROUTE, 4 * CAP_CHUNK), jnp.bfloat16),
        ],
        cost_estimate=SMALL,
        compiler_params=pltpu.CompilerParams(vmem_limit_bytes=4 * 1024 * 1024),
    )(where, own_ids, other_ids, *pieces)


def spread_kernel(where_ref, route, *refs):
    pieces, outs, routed = refs[:4], refs[4:8], refs[8]
    spoken, width = pieces[0].shape[0] - CAP_CHUNK, pieces[0].shape[1]
    total = jnp.dot(route[:, :CAP_CHUNK], pieces[0][spoken:, :], preferred_element_type=jnp.float32)
    for k in range(1, 4):
        columns = slice(k * CAP_CHUNK, (k + 1) * CAP_CHUNK)
        total += jnp.dot(route[:, columns], pieces[k][spoken:, :], preferred_element_type=jnp.float32)
    routed[...] = total.astype(jnp.bfloat16)
    for d, out in enumerate(outs):
        columns = pl.ds(pl.multiple_of(((where_ref[1] + d) & 1) * (width - HALF), 128), HALF)
        for k in range(4):
            low = pl.multiple_of(((where_ref[0] + k) & 3) * spoken, 16)
            out[pl.ds(low, spoken), :] = pieces[k][:spoken, columns]
        out[4 * spoken :, :] = routed[d * CAP_ROUTE : (d + 1) * CAP_ROUTE, columns]


def spread(where, route, pieces):
    tall, width = pieces[0].shape
    rows = 4 * (tall - CAP_CHUNK) + CAP_ROUTE
    return pl.pallas_call(
        spread_kernel,
        in_specs=[pl.BlockSpec(memory_space=pltpu.SMEM)] + [pl.BlockSpec(memory_space=pltpu.VMEM)] * 5,
        out_specs=[pl.BlockSpec(memory_space=pltpu.VMEM)] * 4,
        out_shape=[pltpu.VMEM((rows, HALF), jnp.bfloat16)] * 4,
        scratch_shapes=[pltpu.VMEM((4 * CAP_ROUTE, width), jnp.bfloat16)],
        cost_estimate=SMALL,
        compiler_params=pltpu.CompilerParams(vmem_limit_bytes=6 * 1024 * 1024),
    )(where, route, *pieces)


def join_kernel(first, second, *refs):
    out = refs[-1]
    rows = first.shape[0]
    out[:rows, :] = first[...]
    out[rows:, :] = second[...]


def join(first, second, *order):
    rows, width = first.shape
    vmem = pl.BlockSpec(memory_space=pltpu.VMEM)
    return pl.pallas_call(
        join_kernel,
        in_specs=[vmem, vmem] + [pl.BlockSpec(memory_space=pl.ANY)] * len(order),
        out_specs=vmem,
        out_shape=jax.ShapeDtypeStruct((2 * rows, width), first.dtype),
        cost_estimate=SMALL,
        compiler_params=pltpu.CompilerParams(vmem_limit_bytes=4 * 1024 * 1024),
    )(first, second, *order)


def again_kernel(_, *refs):
    half = len(refs) // 2
    for array, out in zip(refs[:half], refs[half:]):
        out[...] = array[...]


def again(order, *arrays):
    vmem = pl.BlockSpec(memory_space=pltpu.VMEM)
    return pl.pallas_call(
        again_kernel,
        in_specs=[pl.BlockSpec(memory_space=pl.ANY)] + [vmem] * len(arrays),
        out_specs=[vmem] * len(arrays),
        out_shape=[jax.ShapeDtypeStruct(array.shape, array.dtype) for array in arrays],
        cost_estimate=SMALL,
        compiler_params=pltpu.CompilerParams(vmem_limit_bytes=6 * 1024 * 1024),
    )(order, *arrays)


def prepare_kernel(group, where_ref, own_ids, other_ids, *refs):
    logits, weights, flags, largest = refs[:4], refs[4:12], refs[12], refs[13]
    own, other, sems = refs[14:]
    voc = own.shape[1]
    tokens = group // 4
    rows = 2 * group + CAP_ROUTE

    def load(shard):
        pair = logits[2 * shard : 2 * shard + 2]
        return [pltpu.make_async_copy(a, b, sems.at[k]) for k, (a, b) in enumerate(zip(pair, (own, other)))]

    for copy in load(0):
        copy.start()
    ids = by_column(own_ids, other_ids, group)
    spots = ids.shape[1]
    hit = ids < voc * 64
    home = jnp.where(hit, ids // voc, -1)
    z_from, t_from = spots_of(spots, 0)
    z_to, t_to = spots_of(spots, 1)
    place = z_to[:16]
    most = jnp.int32(0)
    for k in range(4):
        excess = jnp.sum(jnp.where(jnp.logical_and(hit, place == k), 1, 0), 1, keepdims=True) - CAP_CHUNK
        most = jnp.maximum(most, jnp.max(excess))
    for k in range(2):
        to_x = jnp.sum(jnp.where(jnp.logical_and(hit, (home >> 3) & 1 == k), 1, 0), 1, keepdims=True)
        to_y = jnp.sum(jnp.where(jnp.logical_and(hit, home >> 5 == k), 1, 0), 1, keepdims=True)
        most = jnp.maximum(most, jnp.max(jnp.maximum(to_x, to_y)) - CAP_ROUTE)
    flags[0] = most
    mine = jnp.where(where_ref[19] == 0, (home >> 3) & 1, home >> 5) == where_ref[16] >> 1
    mine = jnp.logical_and(hit, mine)
    rank = count(mine, jnp.logical_or(z_from < z_to, jnp.logical_and(z_from == z_to, t_from <= t_to)))
    rank = jnp.where(jnp.logical_and(mine, most <= 0), rank, 0)
    number = lax.broadcasted_iota(jnp.int32, (CAP_ROUTE, spots), 0) + 1
    for k in range(2):
        flags[1 + k] = jnp.sum(jnp.where(jnp.logical_and(hit, home * voc == where_ref[17 + k]), 1, 0))

    slots = []
    for c in range(16):
        chosen = rank[c : c + 1, :] == number
        slots.append(jnp.sum(jnp.where(chosen, ids[c : c + 1, :] + 1, 0), 1, keepdims=True) - 1)
    slots = jnp.concatenate(slots, 0)
    for shard in range(2):
        for copy in load(shard):
            copy.wait()
        wide = slice(shard * voc, (shard + 1) * voc)
        columns = lax.broadcasted_iota(jnp.int32, (CAP_ROUTE, voc), 1) + where_ref[17 + shard]
        top = jnp.zeros((8, voc), jnp.float32)
        for n in range(16):
            out, low = weights[n // 2], n % 2 * rows
            at = pl.multiple_of(where_ref[n] * group, 16)
            first, second = own[pl.ds(at, group), :], other[pl.ds(at, group), :]
            for z in range(4):
                both = [array[z * tokens : (z + 1) * tokens, :] for array in (first, second)]
                out[low + 2 * z * tokens : low + 2 * (z + 1) * tokens, wide] = jnp.concatenate(both, 0)
            for array in (first, second):
                size = jnp.abs(array.astype(jnp.float32)).reshape(group // 8, 8, voc)
                top = jnp.maximum(top, jnp.max(size, 0))
            picked = jnp.full((CAP_ROUTE, 1), -1, jnp.int32)
            for c in range(16):
                picked = jnp.where(where_ref[n] == c, slots[c * CAP_ROUTE : (c + 1) * CAP_ROUTE, :], picked)
            out[low + 2 * group : low + rows, wide] = jnp.where(picked == columns, 1.0, 0.0).astype(jnp.bfloat16)
        largest[shard] = jnp.max(top)
        if shard == 0:
            for copy in load(1):
                copy.start()


def prepare(where, own_ids, other_ids, logits, order, group):
    voc = logits[0].shape[1]
    rows = 2 * (2 * group + CAP_ROUTE)
    vmem, smem = pl.BlockSpec(memory_space=pltpu.VMEM), pl.BlockSpec(memory_space=pltpu.SMEM)

    def kernel(where_ref, own_ids, other_ids, *refs):
        prepare_kernel(group, where_ref, own_ids, other_ids, *refs[:4], *refs[5:])

    return pl.pallas_call(
        kernel,
        in_specs=[smem, vmem, vmem] + [pl.BlockSpec(memory_space=pl.ANY)] * 5,
        out_specs=[vmem] * 8 + [smem, smem],
        out_shape=[pltpu.VMEM((rows, 2 * voc), jnp.bfloat16)] * 8
        + [jax.ShapeDtypeStruct((3,), jnp.int32), jax.ShapeDtypeStruct((2,), jnp.float32)],
        scratch_shapes=[pltpu.VMEM(logits[0].shape, logits[0].dtype)] * 2 + [pltpu.SemaphoreType.DMA((2,))],
        cost_estimate=SMALL,
        compiler_params=pltpu.CompilerParams(vmem_limit_bytes=8 * 1024 * 1024),
    )(where, own_ids, other_ids, in_hbm(logits[0]), *logits[1:], order)


def add_products(total, products):
    for weights, rows in products:
        total = total + dot_rows(weights, rows)
    return total


def dot_rows(weights, rows):
    return lax.dot_general(weights, rows, (((0,), (0,)), ((), ())), preferred_element_type=jnp.float32)


def full_embedding(rows, ids, shard, vocab, low):
    tokens = rows.shape[0] // 2
    step = pairs(lambda s, y, x, z, r: (s, (y + (x + (z + 1) // RING) // RING) % RING, (x + (z + 1) // RING) % RING, (z + 1) % RING, r))

    def body(i, state):
        current, total = state
        source = (shard - i) & 63
        here = lax.dynamic_slice_in_dim(ids, source * tokens, tokens, 1).reshape(2 * tokens, 1)
        part = lax.dynamic_slice_in_dim(current, low, HALF, 1)
        return send(current, step), total + dot_rows((here == vocab).astype(jnp.bfloat16), part)

    return lax.fori_loop(0, 64, body, (rows, jnp.zeros((vocab.shape[1], HALF), jnp.float32)))[1]


def local(acts, logit_grad, token_ids, table, moment_one, moment_two):
    section = lax.axis_index("section")
    shard = lax.axis_index("shard")
    rep = lax.axis_index("rep")
    y, x, z_hi = shard >> 4, (shard >> 2) & 3, shard & 3
    on_first = rep == 0
    second, last = pick(on_first, x, y), pick(on_first, y, x)

    own_logits = logit_grad[0]
    assert own_logits.shape[1] == VOC_SHARD
    tokens, model = acts.shape[2:]
    voc = own_logits.shape[1]
    width = model // 4
    part = voc // 4

    pieces = {}
    flips = ((1, 0), (1, 1), (0, 1), (0, 0))
    takers = jnp.stack([2 * (section ^ a) + (rep ^ b) for a, b in flips]).astype(jnp.int32)
    *quarters, own_ids = cut_quarters(takers, token_ids, acts[0, 0])
    for (a, b), block in zip(flips, quarters):
        pieces[a, b] = send(block, quad_pairs(a, b)) if (a, b) != (0, 0) else block

    other_ids = send(own_ids, quad_pairs(0, 1))
    other_logits = send(own_logits, quad_pairs(0, 1))
    logits = [own_logits, other_logits] + [send(array, pair_pairs(0, 0)) for array in (own_logits, other_logits)]

    where = jnp.stack([section, shard >> 2, z_hi, second, rep]).astype(jnp.int32)
    chunk, own_route = build_chunk(where, token_ids, other_ids, [pieces[flip] for flip in flips])

    far, down = (send(chunk, depth_pairs(step)) for step in (2, -1))
    up = send(chunk, depth_pairs(1))

    outgoing = list(spread(jnp.stack([z_hi, second]).astype(jnp.int32), own_route, [chunk, down, far, up]))
    plane = [outgoing[0], *(send(outgoing[k], second_pairs(step)) for k, step in ((3, -1), (2, 2), (1, 1)))]

    partner = pick(on_first, shard ^ 4, shard ^ 16)
    turning = [(second + k) & 3 for k in range(4)]
    order = [((last + offset) & 3, turn) for offset in range(4) for turn in turning]
    places = [pick(on_first, 4 * fixed + turn, 4 * turn + fixed) for fixed, turn in order]
    where = jnp.stack([*places, second, shard * voc, partner * voc, rep]).astype(jnp.int32)
    *weights, flags, largest = prepare(where, token_ids, other_ids, logits, outgoing[1], 4 * tokens)
    weights = [weights[2 * k : 2 * k + 2] for k in range(4)]
    overflow = flags[0] > 0

    places = lax.broadcasted_iota(jnp.int32, (1, voc), 1)
    vocab = jnp.concatenate([shard * voc + places, partner * voc + places], 1)
    def all_rows():
        ids = jnp.concatenate([token_ids, other_ids], 0)
        rows = jnp.concatenate([jnp.where(section == 0, pieces[0, b], pieces[1, b]) for b in (0, 1)], 0)
        return full_embedding(rows, ids, shard, vocab, (second & 1) * (width - HALF))

    start_total = lax.cond(
        overflow,
        all_rows,
        lambda: jnp.zeros((2 * voc, HALF), jnp.float32),
    )

    lower, upper = join(plane[0], plane[1], largest, *plane[2:]), join(plane[2], plane[3], largest, plane[1])
    before, behind = [send(lower, last_pairs(1))], [send(upper, last_pairs(-1))]
    total = add_products(start_total, [(weights[0][0], lower), (weights[0][1], upper)])
    late_lower, late_upper = again(upper, lower, upper)
    before.append(send(late_upper, last_pairs(1)))
    behind.append(send(late_lower, last_pairs(-1)))
    far = send(before[0], last_pairs(1)), send(behind[0], last_pairs(-1))
    total = add_products(total, [(weights[3][0], before[0]), (weights[1][1], behind[0])])
    total = add_products(total, [(weights[3][1], before[1]), (weights[1][0], behind[1])])
    total = add_products(total, [(weights[2][0], far[0]), (weights[2][1], far[1])])

    most = 6.0 * 2 * 64 * tokens
    bound = most * (largest + (flags[1:] > 0).astype(jnp.float32))
    bound = jnp.where(jnp.logical_or(overflow, bound <= 0), 2 * most, bound)
    scale = 32768.0 / bound

    sent = {}
    for a, b, p in ((1, 0, 0), (1, 1, 0), (1, 0, 1), (1, 1, 1), (0, 0, 1), (0, 1, 1), (0, 1, 0), (0, 0, 0)):
        row = p * voc + (2 * (section ^ a) + (rep ^ b)) * part
        block = lax.dynamic_slice_in_dim(total, row, part, 0)
        if a or p:
            block = (block * scale[p]).astype(jnp.float16)
        table_of = pair_pairs(a, b) if p else quad_pairs(a, b)
        sent[a, b, p] = send(block, table_of) if (a, b, p) != (0, 0, 0) else block

    def parts_of(a, b, unscale):
        low_first = pick(rep == b, x, y) & 1 == 0
        here, there = [
            block.astype(jnp.float32) * unscale if block.dtype == jnp.float16 else block
            for block in (sent[a, b, 0], sent[a, b, 1])
        ]
        return [jnp.where(low_first, here, there), jnp.where(low_first, there, here)[:, HALF - PARTS[1] :]]

    state = (table, moment_one, moment_two)
    across = fetch((section ^ 1).reshape(1).astype(jnp.int32), state, sent[0, 1, 0])
    unscale = 1.0 / scale[0]
    near = [2 * section + rep, 2 * section + (rep ^ 1)]
    here = jnp.stack(near * 2).astype(jnp.int32)
    blocks = [parts_of(0, b, unscale) for b in (0, 1)]
    *results, unscale = adamw_pair(here, unscale.reshape(1), *blocks, list(map(in_hbm, state)), None, across[0])
    blocks = [parts_of(1, b, unscale[:1, :1]) for b in (0, 1)]
    there = jnp.stack([2 * (section ^ 1) + rep, 2 * (section ^ 1) + (rep ^ 1), rep, rep ^ 1]).astype(jnp.int32)
    return tuple(adamw_pair(there, 1.0 / scale[:1], *blocks, across, results)[:3])


def solution(mesh):
    rows = P(("shard", "section", "rep"), None)
    return jax.shard_map(
        local,
        mesh=mesh,
        in_specs=(P("section", "rep", "shard", None), P("rep", None, "shard"), P("rep", None), rows, rows, rows),
        out_specs=(rows, rows, rows),
        check_vma=False,
    )
```

```python
import functools

import jax
import jax.numpy as jnp
from jax import lax
from jax.experimental import pallas as pl
from jax.experimental.pallas import tpu as pltpu
from jax.sharding import PartitionSpec as P

corr_first = 1.0 - 0.9**10
corr_second = 1.0 - 0.95**10

AXES = ("section", "shard", "rep")
RING = 4
VOC_SHARD = 384
CAP_CHUNK = 16
CAP_ROUTE = 32
PARTS = (640, 512)
HALF = 640
SMALL = pl.CostEstimate(flops=1024, bytes_accessed=1024, transcendentals=0)


def index_of(section, y, x, z_hi, rep):
    return (section * 64 + (y * RING + x) * RING + z_hi) * 2 + rep


def pairs(move):
    out = []
    for section in range(2):
        for y in range(RING):
            for x in range(RING):
                for z_hi in range(RING):
                    for rep in range(2):
                        out.append((index_of(section, y, x, z_hi, rep), index_of(*move(section, y, x, z_hi, rep))))
    return out


def quad_pairs(a, b):
    return pairs(lambda s, y, x, z, r: (s ^ a, y, x, z, r ^ b))


def depth_pairs(step):
    return pairs(lambda s, y, x, z, r: (s, y, x, (z + step) % RING, r))


def second_pairs(step):
    return pairs(lambda s, y, x, z, r: (s, (y + step * r) % RING, (x + step * (1 - r)) % RING, z, r))


def last_pairs(step):
    return pairs(lambda s, y, x, z, r: (s, (y + step * (1 - r)) % RING, (x + step * r) % RING, z, r))


def pair_pairs(a, b):
    return pairs(lambda s, y, x, z, r: (s ^ a, y ^ r, x ^ (1 - r), z, r ^ b))


def send(array, table):
    return lax.ppermute(array, AXES, table)


def pick(mask, first, second):
    return jnp.where(mask, first, second)


def in_hbm(array):
    return pltpu.with_memory_space_constraint(array, pltpu.HBM)


def adamw_kernel(where_ref, held_ref, *refs):
    parts = len(PARTS)
    firsts, seconds = refs[:parts], refs[parts : 2 * parts]
    t_ref, m_ref, v_ref = refs[2 * parts : 2 * parts + 3]
    t_out, m_out, v_out, held_out = refs[-4:]
    held_out[...] = jnp.full(held_out.shape, held_ref[0], jnp.float32)
    low = 0
    for first, second in zip(firsts, seconds):
        at = (slice(None), slice(low, low + first.shape[1]))
        low += first.shape[1]
        g = jnp.where(pl.program_id(0) == 0, first[...], second[...])
        new_one = 0.9 * m_ref[at] + 0.1 * g
        new_two = 0.95 * v_ref[at] + 0.05 * g * g
        update = new_one / corr_first / (jnp.sqrt(new_two / corr_second) + 1e-08)
        t = t_ref[at]
        t_out[at] = t - 0.01 * (update + 0.1 * t)
        m_out[at] = new_one
        v_out[at] = new_two


def adamw_pair(where, held, first, second, state, previous, *order):
    rows, width = first[0].shape[0], sum(PARTS)
    inner = pl.BlockSpec((rows, width), lambda i, where_ref: (0, where_ref[2 + i]))
    wide = pl.BlockSpec((rows, width), lambda i, where_ref: (0, where_ref[i]))
    small = pl.BlockSpec((1, 1), lambda i, where_ref: (0, 0))
    anywhere = pl.BlockSpec(memory_space=pl.ANY)
    blocks = [*first, *second]
    specs = [pl.BlockSpec(memory_space=pltpu.SMEM)]
    specs += [pl.BlockSpec(block.shape, lambda i, where_ref: (0, 0)) for block in blocks]
    specs += [inner] * 3 + [anywhere] * len(order)
    args = [held, *blocks, *state, *order]
    aliases = {}
    if previous is not None:
        aliases = {1 + len(args) + i: i for i in range(3)}
        specs += [anywhere] * 3
        args += list(previous)
    return pl.pallas_call(
        adamw_kernel,
        grid_spec=pltpu.PrefetchScalarGridSpec(
            num_scalar_prefetch=1, grid=(2,), in_specs=specs, out_specs=[wide] * 3 + [small]
        ),
        out_shape=[jax.ShapeDtypeStruct((rows, 4 * width), jnp.float32)] * 3
        + [jax.ShapeDtypeStruct((1, 1), jnp.float32)],
        input_output_aliases=aliases,
        cost_estimate=SMALL,
        compiler_params=pltpu.CompilerParams(vmem_limit_bytes=10 * 1024 * 1024),
    )(where, *args)


def fetch_kernel(where_ref, *refs):
    sources, outs, sems = refs[:3], refs[4:7], refs[7]
    width = outs[0].shape[1]
    columns = pl.ds(pl.multiple_of(where_ref[0] * width, 128), width)
    copies = [pltpu.make_async_copy(a.at[:, columns], b, sems.at[k]) for k, (a, b) in enumerate(zip(sources, outs))]
    for copy in copies:
        copy.start()
    for copy in copies:
        copy.wait()


def fetch(where, arrays, order):
    anywhere = pl.BlockSpec(memory_space=pl.ANY)
    rows, width = arrays[0].shape
    return pl.pallas_call(
        fetch_kernel,
        in_specs=[pl.BlockSpec(memory_space=pltpu.SMEM)] + [anywhere] * 4,
        out_specs=[pl.BlockSpec(memory_space=pltpu.VMEM)] * 3,
        out_shape=[pltpu.VMEM((rows, width // 2), array.dtype) for array in arrays],
        scratch_shapes=[pltpu.SemaphoreType.DMA((3,))],
        cost_estimate=SMALL,
        compiler_params=pltpu.CompilerParams(vmem_limit_bytes=4 * 1024 * 1024),
    )(where, *map(in_hbm, arrays), order)


def cut_kernel(where_ref, ids, acts, *outs):
    width = outs[0].shape[1]
    for k, out in enumerate(outs[:4]):
        out[...] = acts[:, pl.ds(pl.multiple_of(where_ref[k] * width, 128), width)]
    outs[4][...] = ids[...]


def cut_quarters(where, ids, acts):
    rows, model = acts.shape
    vmem = pl.BlockSpec(memory_space=pltpu.VMEM)
    return pl.pallas_call(
        cut_kernel,
        in_specs=[pl.BlockSpec(memory_space=pltpu.SMEM)] + [vmem] * 2,
        out_specs=[vmem] * 5,
        out_shape=[pltpu.VMEM((rows, model // 4), acts.dtype)] * 4 + [pltpu.VMEM(ids.shape, ids.dtype)],
        cost_estimate=SMALL,
        compiler_params=pltpu.CompilerParams(vmem_limit_bytes=4 * 1024 * 1024),
    )(where, ids, in_hbm(acts))


def by_column(own_ids, other_ids, spots):
    sides = []
    for ids in (own_ids, other_ids):
        sides.append(jnp.concatenate([ids[:, c * spots : (c + 1) * spots] for c in range(16)], 0))
    return jnp.concatenate(sides, 1)


def spots_of(size, dim):
    at = lax.broadcasted_iota(jnp.int32, (size, size), dim)
    side, at = jnp.where(at < size // 2, 0, 1), jnp.where(at < size // 2, at, at - size // 2)
    tokens = size // 8
    z = jnp.where(at < tokens, 0, jnp.where(at < 2 * tokens, 1, jnp.where(at < 3 * tokens, 2, 3)))
    return z, at - z * tokens + side * tokens


def count(flags, upto):
    as_number = lambda mask: jnp.where(mask, 1.0, 0.0).astype(jnp.bfloat16)
    return jnp.dot(as_number(flags), as_number(upto), preferred_element_type=jnp.float32).astype(jnp.int32)


def chunk_kernel(where_ref, own_ids, other_ids, *refs):
    pieces, logits, (chunk, route, copied), (held, sems) = refs[:4], refs[4:6], refs[6:9], refs[9:]
    tall = logits[0].shape[0]
    loads = [pltpu.make_async_copy(array, held.at[k], sems.at[k]) for k, array in enumerate(logits)]
    stores = [pltpu.make_async_copy(held.at[k], copied.at[pl.ds(k * tall, tall)], sems.at[2 + k]) for k in range(2)]
    for load in loads:
        load.start()
    section, column, z_hi, second, rep = (where_ref[k] for k in range(5))
    tokens, width = pieces[0].shape
    here, there = (pieces[3], pieces[2]), (pieces[0], pieces[1])
    hidden = [jnp.where(section == 1, here[b][...], there[b][...]) for b in (0, 1)]
    cotangent = [jnp.where(section == 0, here[b][...], there[b][...]) for b in (0, 1)]
    chunk[: 2 * tokens, :] = jnp.concatenate(hidden, 0)

    for load, store in zip(loads, stores):
        load.wait()
        store.start()
    ids = by_column(own_ids, other_ids, 4 * tokens)
    size = ids.shape[1]
    rows = lax.broadcasted_iota(jnp.int32, ids.shape, 0)
    ids = jnp.sum(jnp.where(rows == column, ids, 0), 0, keepdims=True)
    hit = ids < VOC_SHARD * 64
    home = jnp.where(hit, ids // VOC_SHARD, 0)
    pair = jnp.where(rep == 0, (home >> 3) & 1, home >> 5)
    z_from, t_from = spots_of(size, 0)
    z_to, t_to = spots_of(size, 1)
    in_chunk = jnp.logical_and(z_from == z_to, t_from <= t_to)
    in_column = jnp.logical_or(z_from < z_to, in_chunk)
    eight = lambda row: jnp.broadcast_to(row, (8, size))
    slot = count(eight(hit), in_chunk)[:1]
    as_number = lambda mask: jnp.where(mask, 1.0, 0.0).astype(jnp.bfloat16)

    number = lax.broadcasted_iota(jnp.int32, (CAP_CHUNK, size), 0) + 1
    mine = jnp.logical_and(hit, z_to[:1] == z_hi)
    chosen = as_number(jnp.logical_and(slot == number, mine))
    token = lax.broadcasted_iota(jnp.int32, (size, 2 * tokens), 1)
    token = as_number(token == t_from[:, : 2 * tokens])
    chosen = jnp.dot(chosen, token, preferred_element_type=jnp.float32).astype(jnp.bfloat16)
    both = jnp.concatenate(cotangent, 0)
    chunk[2 * tokens :, :] = jnp.dot(chosen, both, preferred_element_type=jnp.float32).astype(jnp.bfloat16)

    kept = jnp.logical_and(hit, slot <= CAP_CHUNK)
    candidate = ((z_to[:1] - z_hi) & 3) * CAP_CHUNK + slot - 1
    same = lax.broadcasted_iota(jnp.int32, (size, size), 0) == lax.broadcasted_iota(jnp.int32, (size, size), 1)
    candidate = jnp.sum(jnp.where(same, jnp.where(kept, candidate, -1), 0), 1, keepdims=True)
    places = as_number(candidate == lax.broadcasted_iota(jnp.int32, (size, 4 * CAP_CHUNK), 1))
    number = lax.broadcasted_iota(jnp.int32, (CAP_ROUTE, size), 0) + 1
    for d in range(4):
        wanted = jnp.logical_and(kept, pair == ((second + d) & 3) >> 1)
        rank = count(eight(wanted), in_column)[:1]
        going = as_number(jnp.logical_and(rank == number, wanted))
        route[d * CAP_ROUTE : (d + 1) * CAP_ROUTE, :] = jnp.dot(
            going, places, preferred_element_type=jnp.float32
        ).astype(jnp.bfloat16)
    for store in stores:
        store.wait()


def build_chunk(where, own_ids, other_ids, pieces, logits):
    tokens, width = pieces[0].shape
    vmem = pl.BlockSpec(memory_space=pltpu.VMEM)
    return pl.pallas_call(
        chunk_kernel,
        in_specs=[pl.BlockSpec(memory_space=pltpu.SMEM)] + [vmem] * 6 + [pl.BlockSpec(memory_space=pl.ANY)] * 2,
        out_specs=[vmem] * 2 + [pl.BlockSpec(memory_space=pl.ANY)],
        out_shape=[
            jax.ShapeDtypeStruct((2 * tokens + CAP_CHUNK, width), jnp.bfloat16),
            jax.ShapeDtypeStruct((4 * CAP_ROUTE, 4 * CAP_CHUNK), jnp.bfloat16),
            pltpu.HBM((2 * logits[0].shape[0], logits[0].shape[1]), logits[0].dtype),
        ],
        scratch_shapes=[pltpu.VMEM((2, *logits[0].shape), logits[0].dtype), pltpu.SemaphoreType.DMA((4,))],
        cost_estimate=SMALL,
        compiler_params=pltpu.CompilerParams(vmem_limit_bytes=6 * 1024 * 1024),
    )(where, own_ids, other_ids, *pieces, in_hbm(logits[0]), logits[1])


def spread_kernel(where_ref, route, *refs):
    pieces, outs, routed = refs[:4], refs[4:8], refs[8]
    spoken, width = pieces[0].shape[0] - CAP_CHUNK, pieces[0].shape[1]
    total = jnp.dot(route[:, :CAP_CHUNK], pieces[0][spoken:, :], preferred_element_type=jnp.float32)
    for k in range(1, 4):
        columns = slice(k * CAP_CHUNK, (k + 1) * CAP_CHUNK)
        total += jnp.dot(route[:, columns], pieces[k][spoken:, :], preferred_element_type=jnp.float32)
    routed[...] = total.astype(jnp.bfloat16)
    for d, out in enumerate(outs):
        columns = pl.ds(pl.multiple_of(((where_ref[1] + d) & 1) * (width - HALF), 128), HALF)
        for k in range(4):
            low = pl.multiple_of(((where_ref[0] + k) & 3) * spoken, 16)
            out[pl.ds(low, spoken), :] = pieces[k][:spoken, columns]
        out[4 * spoken :, :] = routed[d * CAP_ROUTE : (d + 1) * CAP_ROUTE, columns]


def spread(where, route, pieces):
    tall, width = pieces[0].shape
    rows = 4 * (tall - CAP_CHUNK) + CAP_ROUTE
    return pl.pallas_call(
        spread_kernel,
        in_specs=[pl.BlockSpec(memory_space=pltpu.SMEM)] + [pl.BlockSpec(memory_space=pltpu.VMEM)] * 5,
        out_specs=[pl.BlockSpec(memory_space=pltpu.VMEM)] * 4,
        out_shape=[pltpu.VMEM((rows, HALF), jnp.bfloat16)] * 4,
        scratch_shapes=[pltpu.VMEM((4 * CAP_ROUTE, width), jnp.bfloat16)],
        cost_estimate=SMALL,
        compiler_params=pltpu.CompilerParams(vmem_limit_bytes=6 * 1024 * 1024),
    )(where, route, *pieces)


def join_kernel(first, second, *refs):
    out = refs[-1]
    rows = first.shape[0]
    out[:rows, :] = first[...]
    out[rows:, :] = second[...]


def join(first, second, *order):
    rows, width = first.shape
    vmem = pl.BlockSpec(memory_space=pltpu.VMEM)
    return pl.pallas_call(
        join_kernel,
        in_specs=[vmem, vmem] + [pl.BlockSpec(memory_space=pl.ANY)] * len(order),
        out_specs=vmem,
        out_shape=jax.ShapeDtypeStruct((2 * rows, width), first.dtype),
        cost_estimate=SMALL,
        compiler_params=pltpu.CompilerParams(vmem_limit_bytes=4 * 1024 * 1024),
    )(first, second, *order)


def again_kernel(_, *refs):
    half = len(refs) // 2
    for array, out in zip(refs[:half], refs[half:]):
        out[...] = array[...]


def again(order, *arrays):
    vmem = pl.BlockSpec(memory_space=pltpu.VMEM)
    return pl.pallas_call(
        again_kernel,
        in_specs=[pl.BlockSpec(memory_space=pl.ANY)] + [vmem] * len(arrays),
        out_specs=[vmem] * len(arrays),
        out_shape=[jax.ShapeDtypeStruct(array.shape, array.dtype) for array in arrays],
        cost_estimate=SMALL,
        compiler_params=pltpu.CompilerParams(vmem_limit_bytes=6 * 1024 * 1024),
    )(order, *arrays)


def prepare_kernel(group, where_ref, own_ids, other_ids, *refs):
    logits, weights, flags, largest = refs[:2], refs[2:10], refs[10], refs[11]
    own, other, sems = refs[12:]
    tall = own.shape[0]
    voc = own.shape[1]
    tokens = group // 4
    rows = 2 * group + CAP_ROUTE

    def load(shard):
        pair = [logits[shard].at[pl.ds(k * tall, tall)] for k in range(2)]
        return [pltpu.make_async_copy(a, b, sems.at[k]) for k, (a, b) in enumerate(zip(pair, (own, other)))]

    for copy in load(0):
        copy.start()
    ids = by_column(own_ids, other_ids, group)
    spots = ids.shape[1]
    hit = ids < voc * 64
    home = jnp.where(hit, ids // voc, -1)
    z_from, t_from = spots_of(spots, 0)
    z_to, t_to = spots_of(spots, 1)
    place = z_to[:16]
    most = jnp.int32(0)
    for k in range(4):
        excess = jnp.sum(jnp.where(jnp.logical_and(hit, place == k), 1, 0), 1, keepdims=True) - CAP_CHUNK
        most = jnp.maximum(most, jnp.max(excess))
    for k in range(2):
        to_x = jnp.sum(jnp.where(jnp.logical_and(hit, (home >> 3) & 1 == k), 1, 0), 1, keepdims=True)
        to_y = jnp.sum(jnp.where(jnp.logical_and(hit, home >> 5 == k), 1, 0), 1, keepdims=True)
        most = jnp.maximum(most, jnp.max(jnp.maximum(to_x, to_y)) - CAP_ROUTE)
    flags[0] = most
    mine = jnp.where(where_ref[19] == 0, (home >> 3) & 1, home >> 5) == where_ref[16] >> 1
    mine = jnp.logical_and(hit, mine)
    rank = count(mine, jnp.logical_or(z_from < z_to, jnp.logical_and(z_from == z_to, t_from <= t_to)))
    rank = jnp.where(jnp.logical_and(mine, most <= 0), rank, 0)
    number = lax.broadcasted_iota(jnp.int32, (CAP_ROUTE, spots), 0) + 1
    for k in range(2):
        flags[1 + k] = jnp.sum(jnp.where(jnp.logical_and(hit, home * voc == where_ref[17 + k]), 1, 0))

    slots = []
    for c in range(16):
        chosen = rank[c : c + 1, :] == number
        slots.append(jnp.sum(jnp.where(chosen, ids[c : c + 1, :] + 1, 0), 1, keepdims=True) - 1)
    slots = jnp.concatenate(slots, 0)
    for shard in range(2):
        for copy in load(shard):
            copy.wait()
        wide = slice(shard * voc, (shard + 1) * voc)
        columns = lax.broadcasted_iota(jnp.int32, (CAP_ROUTE, voc), 1) + where_ref[17 + shard]
        top = jnp.zeros((8, voc), jnp.float32)
        for n in range(16):
            out, low = weights[n // 2], n % 2 * rows
            at = pl.multiple_of(where_ref[n] * group, 16)
            first, second = own[pl.ds(at, group), :], other[pl.ds(at, group), :]
            for z in range(4):
                both = [array[z * tokens : (z + 1) * tokens, :] for array in (first, second)]
                out[low + 2 * z * tokens : low + 2 * (z + 1) * tokens, wide] = jnp.concatenate(both, 0)
            for array in (first, second):
                size = jnp.abs(array.astype(jnp.float32)).reshape(group // 8, 8, voc)
                top = jnp.maximum(top, jnp.max(size, 0))
            picked = jnp.full((CAP_ROUTE, 1), -1, jnp.int32)
            for c in range(16):
                picked = jnp.where(where_ref[n] == c, slots[c * CAP_ROUTE : (c + 1) * CAP_ROUTE, :], picked)
            out[low + 2 * group : low + rows, wide] = jnp.where(picked == columns, 1.0, 0.0).astype(jnp.bfloat16)
        largest[shard] = jnp.max(top)
        if shard == 0:
            for copy in load(1):
                copy.start()


def prepare(where, own_ids, other_ids, logits, order, group):
    voc = logits[0].shape[1]
    rows = 2 * (2 * group + CAP_ROUTE)
    vmem, smem = pl.BlockSpec(memory_space=pltpu.VMEM), pl.BlockSpec(memory_space=pltpu.SMEM)

    def kernel(where_ref, own_ids, other_ids, *refs):
        prepare_kernel(group, where_ref, own_ids, other_ids, *refs[:2], *refs[3:])

    return pl.pallas_call(
        kernel,
        in_specs=[smem, vmem, vmem] + [pl.BlockSpec(memory_space=pl.ANY)] * 3,
        out_specs=[vmem] * 8 + [smem, smem],
        out_shape=[pltpu.VMEM((rows, 2 * voc), jnp.bfloat16)] * 8
        + [jax.ShapeDtypeStruct((3,), jnp.int32), jax.ShapeDtypeStruct((2,), jnp.float32)],
        scratch_shapes=[pltpu.VMEM((logits[0].shape[0] // 2, voc), logits[0].dtype)] * 2
        + [pltpu.SemaphoreType.DMA((2,))],
        cost_estimate=SMALL,
        compiler_params=pltpu.CompilerParams(vmem_limit_bytes=8 * 1024 * 1024),
    )(where, own_ids, other_ids, *logits, order)


def add_products(total, products):
    for weights, rows in products:
        total = total + dot_rows(weights, rows)
    return total


def dot_rows(weights, rows):
    return lax.dot_general(weights, rows, (((0,), (0,)), ((), ())), preferred_element_type=jnp.float32)


def full_embedding(rows, ids, shard, vocab, low):
    tokens = rows.shape[0] // 2
    step = pairs(lambda s, y, x, z, r: (s, (y + (x + (z + 1) // RING) // RING) % RING, (x + (z + 1) // RING) % RING, (z + 1) % RING, r))

    def body(i, state):
        current, total = state
        source = (shard - i) & 63
        here = lax.dynamic_slice_in_dim(ids, source * tokens, tokens, 1).reshape(2 * tokens, 1)
        part = lax.dynamic_slice_in_dim(current, low, HALF, 1)
        return send(current, step), total + dot_rows((here == vocab).astype(jnp.bfloat16), part)

    return lax.fori_loop(0, 64, body, (rows, jnp.zeros((vocab.shape[1], HALF), jnp.float32)))[1]


def local(acts, logit_grad, token_ids, table, moment_one, moment_two):
    section = lax.axis_index("section")
    shard = lax.axis_index("shard")
    rep = lax.axis_index("rep")
    y, x, z_hi = shard >> 4, (shard >> 2) & 3, shard & 3
    on_first = rep == 0
    second, last = pick(on_first, x, y), pick(on_first, y, x)

    own_logits = logit_grad[0]
    assert own_logits.shape[1] == VOC_SHARD
    tokens, model = acts.shape[2:]
    voc = own_logits.shape[1]
    width = model // 4
    part = voc // 4

    pieces = {}
    flips = ((1, 0), (1, 1), (0, 1), (0, 0))
    takers = jnp.stack([2 * (section ^ a) + (rep ^ b) for a, b in flips]).astype(jnp.int32)
    *quarters, own_ids = cut_quarters(takers, token_ids, acts[0, 0])
    for (a, b), block in zip(flips, quarters):
        pieces[a, b] = send(block, quad_pairs(a, b)) if (a, b) != (0, 0) else block

    other_ids = send(own_ids, quad_pairs(0, 1))
    other_logits = send(own_logits, quad_pairs(0, 1))

    where = jnp.stack([section, shard >> 2, z_hi, second, rep]).astype(jnp.int32)
    chunk, own_route, both = build_chunk(
        where, token_ids, other_ids, [pieces[flip] for flip in flips], [own_logits, other_logits]
    )
    logits = [both, send(both, pair_pairs(0, 0))]

    far, down = (send(chunk, depth_pairs(step)) for step in (2, -1))
    up = send(chunk, depth_pairs(1))

    outgoing = list(spread(jnp.stack([z_hi, second]).astype(jnp.int32), own_route, [chunk, down, far, up]))
    plane = [outgoing[0], *(send(outgoing[k], second_pairs(step)) for k, step in ((3, -1), (2, 2), (1, 1)))]

    partner = pick(on_first, shard ^ 4, shard ^ 16)
    turning = [(second + k) & 3 for k in range(4)]
    order = [((last + offset) & 3, turn) for offset in range(4) for turn in turning]
    places = [pick(on_first, 4 * fixed + turn, 4 * turn + fixed) for fixed, turn in order]
    where = jnp.stack([*places, second, shard * voc, partner * voc, rep]).astype(jnp.int32)
    *weights, flags, largest = prepare(where, token_ids, other_ids, logits, outgoing[1], 4 * tokens)
    weights = [weights[2 * k : 2 * k + 2] for k in range(4)]
    overflow = flags[0] > 0

    places = lax.broadcasted_iota(jnp.int32, (1, voc), 1)
    vocab = jnp.concatenate([shard * voc + places, partner * voc + places], 1)
    def all_rows():
        ids = jnp.concatenate([token_ids, other_ids], 0)
        rows = jnp.concatenate([jnp.where(section == 0, pieces[0, b], pieces[1, b]) for b in (0, 1)], 0)
        return full_embedding(rows, ids, shard, vocab, (second & 1) * (width - HALF))

    start_total = lax.cond(
        overflow,
        all_rows,
        lambda: jnp.zeros((2 * voc, HALF), jnp.float32),
    )

    lower, upper = join(plane[0], plane[1], largest, *plane[2:]), join(plane[2], plane[3], largest, plane[1])
    before, behind = [send(lower, last_pairs(1))], [send(upper, last_pairs(-1))]
    total = add_products(start_total, [(weights[0][0], lower), (weights[0][1], upper)])
    late_lower, late_upper = again(upper, lower, upper)
    before.append(send(late_upper, last_pairs(1)))
    behind.append(send(late_lower, last_pairs(-1)))
    far = send(before[0], last_pairs(1)), send(behind[0], last_pairs(-1))
    total = add_products(total, [(weights[3][0], before[0]), (weights[1][1], behind[0])])
    total = add_products(total, [(weights[3][1], before[1]), (weights[1][0], behind[1])])
    total = add_products(total, [(weights[2][0], far[0]), (weights[2][1], far[1])])

    most = 6.0 * 2 * 64 * tokens
    bound = most * (largest + (flags[1:] > 0).astype(jnp.float32))
    bound = jnp.where(jnp.logical_or(overflow, bound <= 0), 2 * most, bound)
    scale = 32768.0 / bound

    sent = {}
    for a, b, p in ((1, 0, 0), (1, 1, 0), (1, 0, 1), (1, 1, 1), (0, 0, 1), (0, 1, 1), (0, 1, 0), (0, 0, 0)):
        row = p * voc + (2 * (section ^ a) + (rep ^ b)) * part
        block = lax.dynamic_slice_in_dim(total, row, part, 0)
        if a or p:
            block = (block * scale[p]).astype(jnp.float16)
        table_of = pair_pairs(a, b) if p else quad_pairs(a, b)
        sent[a, b, p] = send(block, table_of) if (a, b, p) != (0, 0, 0) else block

    def parts_of(a, b, unscale):
        low_first = pick(rep == b, x, y) & 1 == 0
        here, there = [
            block.astype(jnp.float32) * unscale if block.dtype == jnp.float16 else block
            for block in (sent[a, b, 0], sent[a, b, 1])
        ]
        return [jnp.where(low_first, here, there), jnp.where(low_first, there, here)[:, HALF - PARTS[1] :]]

    state = (table, moment_one, moment_two)
    across = fetch((section ^ 1).reshape(1).astype(jnp.int32), state, sent[0, 1, 0])
    unscale = 1.0 / scale[0]
    near = [2 * section + rep, 2 * section + (rep ^ 1)]
    here = jnp.stack(near * 2).astype(jnp.int32)
    blocks = [parts_of(0, b, unscale) for b in (0, 1)]
    *results, unscale = adamw_pair(here, unscale.reshape(1), *blocks, list(map(in_hbm, state)), None, across[0])
    blocks = [parts_of(1, b, unscale) for b in (0, 1)]
    there = jnp.stack([2 * (section ^ 1) + rep, 2 * (section ^ 1) + (rep ^ 1), rep, rep ^ 1]).astype(jnp.int32)
    return tuple(adamw_pair(there, 1.0 / scale[:1], *blocks, across, results)[:3])


def solution(mesh):
    rows = P(("shard", "section", "rep"), None)
    return jax.shard_map(
        local,
        mesh=mesh,
        in_specs=(P("section", "rep", "shard", None), P("rep", None, "shard"), P("rep", None), rows, rows, rows),
        out_specs=(rows, rows, rows),
        check_vma=False,
    )
```

```python
import functools

import jax
import jax.numpy as jnp
from jax import lax
from jax.experimental import pallas as pl
from jax.experimental.pallas import tpu as pltpu
from jax.sharding import PartitionSpec as P

corr_first = 1.0 - 0.9**10
corr_second = 1.0 - 0.95**10

AXES = ("section", "shard", "rep")
RING = 4
VOC_SHARD = 384
CAP_CHUNK = 16
CAP_ROUTE = 32
PARTS = (640, 512)
HALF = 640
SMALL = pl.CostEstimate(flops=1024, bytes_accessed=1024, transcendentals=0)


def index_of(section, y, x, z_hi, rep):
    return (section * 64 + (y * RING + x) * RING + z_hi) * 2 + rep


def pairs(move):
    out = []
    for section in range(2):
        for y in range(RING):
            for x in range(RING):
                for z_hi in range(RING):
                    for rep in range(2):
                        out.append((index_of(section, y, x, z_hi, rep), index_of(*move(section, y, x, z_hi, rep))))
    return out


def quad_pairs(a, b):
    return pairs(lambda s, y, x, z, r: (s ^ a, y, x, z, r ^ b))


def depth_pairs(step):
    return pairs(lambda s, y, x, z, r: (s, y, x, (z + step) % RING, r))


def second_pairs(step):
    return pairs(lambda s, y, x, z, r: (s, (y + step * r) % RING, (x + step * (1 - r)) % RING, z, r))


def last_pairs(step):
    return pairs(lambda s, y, x, z, r: (s, (y + step * (1 - r)) % RING, (x + step * r) % RING, z, r))


def pair_pairs(a, b):
    return pairs(lambda s, y, x, z, r: (s ^ a, y ^ r, x ^ (1 - r), z, r ^ b))


def send(array, table):
    return lax.ppermute(array, AXES, table)


def pick(mask, first, second):
    return jnp.where(mask, first, second)


def in_hbm(array):
    return pltpu.with_memory_space_constraint(array, pltpu.HBM)


def adamw_kernel(where_ref, held_ref, *refs):
    parts = len(PARTS)
    firsts, seconds = refs[:parts], refs[parts : 2 * parts]
    t_ref, m_ref, v_ref = refs[2 * parts : 2 * parts + 3]
    t_out, m_out, v_out, held_out = refs[-4:]
    held_out[...] = jnp.full(held_out.shape, held_ref[0], jnp.float32)
    low = 0
    for first, second in zip(firsts, seconds):
        at = (slice(None), slice(low, low + first.shape[1]))
        low += first.shape[1]
        g = jnp.where(pl.program_id(0) == 0, first[...], second[...])
        new_one = 0.9 * m_ref[at] + 0.1 * g
        new_two = 0.95 * v_ref[at] + 0.05 * g * g
        update = new_one / corr_first / (jnp.sqrt(new_two / corr_second) + 1e-08)
        t = t_ref[at]
        t_out[at] = t - 0.01 * (update + 0.1 * t)
        m_out[at] = new_one
        v_out[at] = new_two


def adamw_pair(where, held, first, second, state, previous, *order):
    rows, width = first[0].shape[0], sum(PARTS)
    inner = pl.BlockSpec((rows, width), lambda i, where_ref: (0, where_ref[2 + i]))
    wide = pl.BlockSpec((rows, width), lambda i, where_ref: (0, where_ref[i]))
    small = pl.BlockSpec((1, 1), lambda i, where_ref: (0, 0))
    anywhere = pl.BlockSpec(memory_space=pl.ANY)
    blocks = [*first, *second]
    specs = [pl.BlockSpec(memory_space=pltpu.SMEM)]
    specs += [pl.BlockSpec(block.shape, lambda i, where_ref: (0, 0)) for block in blocks]
    specs += [inner] * 3 + [anywhere] * len(order)
    args = [held, *blocks, *state, *order]
    aliases = {}
    if previous is not None:
        aliases = {1 + len(args) + i: i for i in range(3)}
        specs += [anywhere] * 3
        args += list(previous)
    return pl.pallas_call(
        adamw_kernel,
        grid_spec=pltpu.PrefetchScalarGridSpec(
            num_scalar_prefetch=1, grid=(2,), in_specs=specs, out_specs=[wide] * 3 + [small]
        ),
        out_shape=[jax.ShapeDtypeStruct((rows, 4 * width), jnp.float32)] * 3
        + [jax.ShapeDtypeStruct((1, 1), jnp.float32)],
        input_output_aliases=aliases,
        cost_estimate=SMALL,
        compiler_params=pltpu.CompilerParams(vmem_limit_bytes=10 * 1024 * 1024),
    )(where, *args)


def fetch_kernel(where_ref, *refs):
    sources, outs, sems = refs[:3], refs[4:7], refs[7]
    width = outs[0].shape[1]
    columns = pl.ds(pl.multiple_of(where_ref[0] * width, 128), width)
    copies = [pltpu.make_async_copy(a.at[:, columns], b, sems.at[k]) for k, (a, b) in enumerate(zip(sources, outs))]
    for copy in copies:
        copy.start()
    for copy in copies:
        copy.wait()


def fetch(where, arrays, order):
    anywhere = pl.BlockSpec(memory_space=pl.ANY)
    rows, width = arrays[0].shape
    return pl.pallas_call(
        fetch_kernel,
        in_specs=[pl.BlockSpec(memory_space=pltpu.SMEM)] + [anywhere] * 4,
        out_specs=[pl.BlockSpec(memory_space=pltpu.VMEM)] * 3,
        out_shape=[pltpu.VMEM((rows, width // 2), array.dtype) for array in arrays],
        scratch_shapes=[pltpu.SemaphoreType.DMA((3,))],
        cost_estimate=SMALL,
        compiler_params=pltpu.CompilerParams(vmem_limit_bytes=4 * 1024 * 1024),
    )(where, *map(in_hbm, arrays), order)


def cut_kernel(where_ref, ids, acts, *outs):
    width = outs[0].shape[1]
    for k, out in enumerate(outs[:4]):
        out[...] = acts[:, pl.ds(pl.multiple_of(where_ref[k] * width, 128), width)]
    outs[4][...] = ids[...]


def cut_quarters(where, ids, acts):
    rows, model = acts.shape
    vmem = pl.BlockSpec(memory_space=pltpu.VMEM)
    return pl.pallas_call(
        cut_kernel,
        in_specs=[pl.BlockSpec(memory_space=pltpu.SMEM)] + [vmem] * 2,
        out_specs=[vmem] * 5,
        out_shape=[pltpu.VMEM((rows, model // 4), acts.dtype)] * 4 + [pltpu.VMEM(ids.shape, ids.dtype)],
        cost_estimate=SMALL,
        compiler_params=pltpu.CompilerParams(vmem_limit_bytes=4 * 1024 * 1024),
    )(where, ids, in_hbm(acts))


def by_column(own_ids, other_ids, spots):
    sides = []
    for ids in (own_ids, other_ids):
        sides.append(jnp.concatenate([ids[:, c * spots : (c + 1) * spots] for c in range(16)], 0))
    return jnp.concatenate(sides, 1)


def spots_of(size, dim):
    at = lax.broadcasted_iota(jnp.int32, (size, size), dim)
    side, at = jnp.where(at < size // 2, 0, 1), jnp.where(at < size // 2, at, at - size // 2)
    tokens = size // 8
    z = jnp.where(at < tokens, 0, jnp.where(at < 2 * tokens, 1, jnp.where(at < 3 * tokens, 2, 3)))
    return z, at - z * tokens + side * tokens


def count(flags, upto):
    as_number = lambda mask: jnp.where(mask, 1.0, 0.0).astype(jnp.bfloat16)
    return jnp.dot(as_number(flags), as_number(upto), preferred_element_type=jnp.float32).astype(jnp.int32)


def chunk_kernel(where_ref, own_ids, other_ids, *refs):
    pieces, logits, (chunk, route, copied), (held, sems) = refs[:4], refs[4:6], refs[6:9], refs[9:]
    tall = logits[0].shape[0]
    loads = [pltpu.make_async_copy(array, held.at[k], sems.at[k]) for k, array in enumerate(logits)]
    stores = [pltpu.make_async_copy(held.at[k], copied.at[pl.ds(k * tall, tall)], sems.at[2 + k]) for k in range(2)]
    for load in loads:
        load.start()
    section, column, z_hi, second, rep = (where_ref[k] for k in range(5))
    tokens, width = pieces[0].shape
    here, there = (pieces[3], pieces[2]), (pieces[0], pieces[1])
    hidden = [jnp.where(section == 1, here[b][...], there[b][...]) for b in (0, 1)]
    cotangent = [jnp.where(section == 0, here[b][...], there[b][...]) for b in (0, 1)]
    chunk[: 2 * tokens, :] = jnp.concatenate(hidden, 0)

    for load, store in zip(loads, stores):
        load.wait()
        store.start()
    ids = by_column(own_ids, other_ids, 4 * tokens)
    size = ids.shape[1]
    rows = lax.broadcasted_iota(jnp.int32, ids.shape, 0)
    ids = jnp.sum(jnp.where(rows == column, ids, 0), 0, keepdims=True)
    hit = ids < VOC_SHARD * 64
    home = jnp.where(hit, ids // VOC_SHARD, 0)
    pair = jnp.where(rep == 0, (home >> 3) & 1, home >> 5)
    z_from, t_from = spots_of(size, 0)
    z_to, t_to = spots_of(size, 1)
    in_chunk = jnp.logical_and(z_from == z_to, t_from <= t_to)
    in_column = jnp.logical_or(z_from < z_to, in_chunk)
    eight = lambda row: jnp.broadcast_to(row, (8, size))
    slot = count(eight(hit), in_chunk)[:1]
    as_number = lambda mask: jnp.where(mask, 1.0, 0.0).astype(jnp.bfloat16)

    number = lax.broadcasted_iota(jnp.int32, (CAP_CHUNK, size), 0) + 1
    mine = jnp.logical_and(hit, z_to[:1] == z_hi)
    chosen = as_number(jnp.logical_and(slot == number, mine))
    token = lax.broadcasted_iota(jnp.int32, (size, 2 * tokens), 1)
    token = as_number(token == t_from[:, : 2 * tokens])
    chosen = jnp.dot(chosen, token, preferred_element_type=jnp.float32).astype(jnp.bfloat16)
    both = jnp.concatenate(cotangent, 0)
    chunk[2 * tokens :, :] = jnp.dot(chosen, both, preferred_element_type=jnp.float32).astype(jnp.bfloat16)

    kept = jnp.logical_and(hit, slot <= CAP_CHUNK)
    candidate = ((z_to[:1] - z_hi) & 3) * CAP_CHUNK + slot - 1
    same = lax.broadcasted_iota(jnp.int32, (size, size), 0) == lax.broadcasted_iota(jnp.int32, (size, size), 1)
    candidate = jnp.sum(jnp.where(same, jnp.where(kept, candidate, -1), 0), 1, keepdims=True)
    places = as_number(candidate == lax.broadcasted_iota(jnp.int32, (size, 4 * CAP_CHUNK), 1))
    number = lax.broadcasted_iota(jnp.int32, (CAP_ROUTE, size), 0) + 1
    for d in range(4):
        wanted = jnp.logical_and(kept, pair == ((second + d) & 3) >> 1)
        rank = count(eight(wanted), in_column)[:1]
        going = as_number(jnp.logical_and(rank == number, wanted))
        route[d * CAP_ROUTE : (d + 1) * CAP_ROUTE, :] = jnp.dot(
            going, places, preferred_element_type=jnp.float32
        ).astype(jnp.bfloat16)
    for store in stores:
        store.wait()


def build_chunk(where, own_ids, other_ids, pieces, logits):
    tokens, width = pieces[0].shape
    vmem = pl.BlockSpec(memory_space=pltpu.VMEM)
    return pl.pallas_call(
        chunk_kernel,
        in_specs=[pl.BlockSpec(memory_space=pltpu.SMEM)] + [vmem] * 6 + [pl.BlockSpec(memory_space=pl.ANY)] * 2,
        out_specs=[vmem] * 2 + [pl.BlockSpec(memory_space=pl.ANY)],
        out_shape=[
            jax.ShapeDtypeStruct((2 * tokens + CAP_CHUNK, width), jnp.bfloat16),
            jax.ShapeDtypeStruct((4 * CAP_ROUTE, 4 * CAP_CHUNK), jnp.bfloat16),
            pltpu.HBM((2 * logits[0].shape[0], logits[0].shape[1]), logits[0].dtype),
        ],
        scratch_shapes=[pltpu.VMEM((2, *logits[0].shape), logits[0].dtype), pltpu.SemaphoreType.DMA((4,))],
        cost_estimate=SMALL,
        compiler_params=pltpu.CompilerParams(vmem_limit_bytes=6 * 1024 * 1024),
    )(where, own_ids, other_ids, *pieces, in_hbm(logits[0]), logits[1])


def spread_kernel(where_ref, route, *refs):
    pieces, outs, routed = refs[:4], refs[4:8], refs[8]
    spoken, width = pieces[0].shape[0] - CAP_CHUNK, pieces[0].shape[1]
    total = jnp.dot(route[:, :CAP_CHUNK], pieces[0][spoken:, :], preferred_element_type=jnp.float32)
    for k in range(1, 4):
        columns = slice(k * CAP_CHUNK, (k + 1) * CAP_CHUNK)
        total += jnp.dot(route[:, columns], pieces[k][spoken:, :], preferred_element_type=jnp.float32)
    routed[...] = total.astype(jnp.bfloat16)
    for d, out in enumerate(outs):
        columns = pl.ds(pl.multiple_of(((where_ref[1] + d) & 1) * (width - HALF), 128), HALF)
        for k in range(4):
            low = pl.multiple_of(((where_ref[0] + k) & 3) * spoken, 16)
            out[pl.ds(low, spoken), :] = pieces[k][:spoken, columns]
        out[4 * spoken :, :] = routed[d * CAP_ROUTE : (d + 1) * CAP_ROUTE, columns]


def spread(where, route, pieces):
    tall, width = pieces[0].shape
    rows = 4 * (tall - CAP_CHUNK) + CAP_ROUTE
    return pl.pallas_call(
        spread_kernel,
        in_specs=[pl.BlockSpec(memory_space=pltpu.SMEM)] + [pl.BlockSpec(memory_space=pltpu.VMEM)] * 5,
        out_specs=[pl.BlockSpec(memory_space=pltpu.VMEM)] * 4,
        out_shape=[pltpu.VMEM((rows, HALF), jnp.bfloat16)] * 4,
        scratch_shapes=[pltpu.VMEM((4 * CAP_ROUTE, width), jnp.bfloat16)],
        cost_estimate=SMALL,
        compiler_params=pltpu.CompilerParams(vmem_limit_bytes=6 * 1024 * 1024),
    )(where, route, *pieces)


def join_kernel(first, second, *refs):
    out = refs[-1]
    rows = first.shape[0]
    out[:rows, :] = first[...]
    out[rows:, :] = second[...]


def join(first, second, *order):
    rows, width = first.shape
    vmem = pl.BlockSpec(memory_space=pltpu.VMEM)
    return pl.pallas_call(
        join_kernel,
        in_specs=[vmem, vmem] + [pl.BlockSpec(memory_space=pl.ANY)] * len(order),
        out_specs=vmem,
        out_shape=jax.ShapeDtypeStruct((2 * rows, width), first.dtype),
        cost_estimate=SMALL,
        compiler_params=pltpu.CompilerParams(vmem_limit_bytes=4 * 1024 * 1024),
    )(first, second, *order)


def again_kernel(_, *refs):
    half = len(refs) // 2
    for array, out in zip(refs[:half], refs[half:]):
        out[...] = array[...]


def again(order, *arrays):
    vmem = pl.BlockSpec(memory_space=pltpu.VMEM)
    return pl.pallas_call(
        again_kernel,
        in_specs=[pl.BlockSpec(memory_space=pl.ANY)] + [vmem] * len(arrays),
        out_specs=[vmem] * len(arrays),
        out_shape=[jax.ShapeDtypeStruct(array.shape, array.dtype) for array in arrays],
        cost_estimate=SMALL,
        compiler_params=pltpu.CompilerParams(vmem_limit_bytes=6 * 1024 * 1024),
    )(order, *arrays)


def prepare_kernel(group, where_ref, own_ids, other_ids, *refs):
    logits, weights, flags, largest = refs[:2], refs[2:10], refs[10], refs[11]
    own, other, sems = refs[12:]
    tall = own.shape[0]
    voc = own.shape[1]
    tokens = group // 4
    rows = 2 * group + CAP_ROUTE

    halves = [[array.at[pl.ds(k * tall, tall)] for k in range(2)] for array in logits]
    copies = [pltpu.make_async_copy(a, b, sems.at[k]) for k, (a, b) in enumerate(zip(halves[0], (own, other)))]
    for copy in copies:
        copy.start()
    ids = by_column(own_ids, other_ids, group)
    spots = ids.shape[1]
    hit = ids < voc * 64
    home = jnp.where(hit, ids // voc, -1)
    z_from, t_from = spots_of(spots, 0)
    z_to, t_to = spots_of(spots, 1)
    place = z_to[:16]
    most = jnp.int32(0)
    for k in range(4):
        excess = jnp.sum(jnp.where(jnp.logical_and(hit, place == k), 1, 0), 1, keepdims=True) - CAP_CHUNK
        most = jnp.maximum(most, jnp.max(excess))
    for k in range(2):
        to_x = jnp.sum(jnp.where(jnp.logical_and(hit, (home >> 3) & 1 == k), 1, 0), 1, keepdims=True)
        to_y = jnp.sum(jnp.where(jnp.logical_and(hit, home >> 5 == k), 1, 0), 1, keepdims=True)
        most = jnp.maximum(most, jnp.max(jnp.maximum(to_x, to_y)) - CAP_ROUTE)
    flags[0] = most
    mine = jnp.where(where_ref[19] == 0, (home >> 3) & 1, home >> 5) == where_ref[16] >> 1
    mine = jnp.logical_and(hit, mine)
    rank = count(mine, jnp.logical_or(z_from < z_to, jnp.logical_and(z_from == z_to, t_from <= t_to)))
    rank = jnp.where(jnp.logical_and(mine, most <= 0), rank, 0)
    number = lax.broadcasted_iota(jnp.int32, (CAP_ROUTE, spots), 0) + 1
    for k in range(2):
        flags[1 + k] = jnp.sum(jnp.where(jnp.logical_and(hit, home * voc == where_ref[17 + k]), 1, 0))

    slots = []
    for c in range(16):
        chosen = rank[c : c + 1, :] == number
        slots.append(jnp.sum(jnp.where(chosen, ids[c : c + 1, :] + 1, 0), 1, keepdims=True) - 1)
    slots = jnp.concatenate(slots, 0)
    for shard in range(2):
        sides = (own, other) if shard == 0 else halves[1]
        if shard == 0:
            for copy in copies:
                copy.wait()
        wide = slice(shard * voc, (shard + 1) * voc)
        columns = lax.broadcasted_iota(jnp.int32, (CAP_ROUTE, voc), 1) + where_ref[17 + shard]
        top = jnp.zeros((8, voc), jnp.float32)
        for n in range(16):
            out, low = weights[n // 2], n % 2 * rows
            at = pl.multiple_of(where_ref[n] * group, 16)
            first, second = [side[pl.ds(at, group), :] for side in sides]
            for z in range(4):
                both = [array[z * tokens : (z + 1) * tokens, :] for array in (first, second)]
                out[low + 2 * z * tokens : low + 2 * (z + 1) * tokens, wide] = jnp.concatenate(both, 0)
            for array in (first, second):
                size = jnp.abs(array.astype(jnp.float32)).reshape(group // 8, 8, voc)
                top = jnp.maximum(top, jnp.max(size, 0))
            picked = jnp.full((CAP_ROUTE, 1), -1, jnp.int32)
            for c in range(16):
                picked = jnp.where(where_ref[n] == c, slots[c * CAP_ROUTE : (c + 1) * CAP_ROUTE, :], picked)
            out[low + 2 * group : low + rows, wide] = jnp.where(picked == columns, 1.0, 0.0).astype(jnp.bfloat16)
        largest[shard] = jnp.max(top)


def prepare(where, own_ids, other_ids, logits, order, group):
    voc = logits[0].shape[1]
    rows = 2 * (2 * group + CAP_ROUTE)
    vmem, smem = pl.BlockSpec(memory_space=pltpu.VMEM), pl.BlockSpec(memory_space=pltpu.SMEM)

    def kernel(where_ref, own_ids, other_ids, *refs):
        prepare_kernel(group, where_ref, own_ids, other_ids, *refs[:2], *refs[3:])

    return pl.pallas_call(
        kernel,
        in_specs=[smem, vmem, vmem, pl.BlockSpec(memory_space=pl.ANY), vmem, pl.BlockSpec(memory_space=pl.ANY)],
        out_specs=[vmem] * 8 + [smem, smem],
        out_shape=[pltpu.VMEM((rows, 2 * voc), jnp.bfloat16)] * 8
        + [jax.ShapeDtypeStruct((3,), jnp.int32), jax.ShapeDtypeStruct((2,), jnp.float32)],
        scratch_shapes=[pltpu.VMEM((logits[0].shape[0] // 2, voc), logits[0].dtype)] * 2
        + [pltpu.SemaphoreType.DMA((2,))],
        cost_estimate=SMALL,
        compiler_params=pltpu.CompilerParams(vmem_limit_bytes=8 * 1024 * 1024),
    )(where, own_ids, other_ids, in_hbm(logits[0]), logits[1], order)


def add_products(total, products):
    for weights, rows in products:
        total = total + dot_rows(weights, rows)
    return total


def dot_rows(weights, rows):
    return lax.dot_general(weights, rows, (((0,), (0,)), ((), ())), preferred_element_type=jnp.float32)


def full_embedding(rows, ids, shard, vocab, low):
    tokens = rows.shape[0] // 2
    step = pairs(lambda s, y, x, z, r: (s, (y + (x + (z + 1) // RING) // RING) % RING, (x + (z + 1) // RING) % RING, (z + 1) % RING, r))

    def body(i, state):
        current, total = state
        source = (shard - i) & 63
        here = lax.dynamic_slice_in_dim(ids, source * tokens, tokens, 1).reshape(2 * tokens, 1)
        part = lax.dynamic_slice_in_dim(current, low, HALF, 1)
        return send(current, step), total + dot_rows((here == vocab).astype(jnp.bfloat16), part)

    return lax.fori_loop(0, 64, body, (rows, jnp.zeros((vocab.shape[1], HALF), jnp.float32)))[1]


def local(acts, logit_grad, token_ids, table, moment_one, moment_two):
    section = lax.axis_index("section")
    shard = lax.axis_index("shard")
    rep = lax.axis_index("rep")
    y, x, z_hi = shard >> 4, (shard >> 2) & 3, shard & 3
    on_first = rep == 0
    second, last = pick(on_first, x, y), pick(on_first, y, x)

    own_logits = logit_grad[0]
    assert own_logits.shape[1] == VOC_SHARD
    tokens, model = acts.shape[2:]
    voc = own_logits.shape[1]
    width = model // 4
    part = voc // 4

    pieces = {}
    flips = ((1, 0), (1, 1), (0, 1), (0, 0))
    takers = jnp.stack([2 * (section ^ a) + (rep ^ b) for a, b in flips]).astype(jnp.int32)
    *quarters, own_ids = cut_quarters(takers, token_ids, acts[0, 0])
    for (a, b), block in zip(flips, quarters):
        pieces[a, b] = send(block, quad_pairs(a, b)) if (a, b) != (0, 0) else block

    other_ids = send(own_ids, quad_pairs(0, 1))
    other_logits = send(own_logits, quad_pairs(0, 1))

    where = jnp.stack([section, shard >> 2, z_hi, second, rep]).astype(jnp.int32)
    chunk, own_route, both = build_chunk(
        where, token_ids, other_ids, [pieces[flip] for flip in flips], [own_logits, other_logits]
    )
    logits = [both, send(both, pair_pairs(0, 0))]

    far, down = (send(chunk, depth_pairs(step)) for step in (2, -1))
    up = send(chunk, depth_pairs(1))

    outgoing = list(spread(jnp.stack([z_hi, second]).astype(jnp.int32), own_route, [chunk, down, far, up]))
    plane = [outgoing[0], *(send(outgoing[k], second_pairs(step)) for k, step in ((3, -1), (2, 2), (1, 1)))]

    partner = pick(on_first, shard ^ 4, shard ^ 16)
    turning = [(second + k) & 3 for k in range(4)]
    order = [((last + offset) & 3, turn) for offset in range(4) for turn in turning]
    places = [pick(on_first, 4 * fixed + turn, 4 * turn + fixed) for fixed, turn in order]
    where = jnp.stack([*places, second, shard * voc, partner * voc, rep]).astype(jnp.int32)
    *weights, flags, largest = prepare(where, token_ids, other_ids, logits, outgoing[1], 4 * tokens)
    weights = [weights[2 * k : 2 * k + 2] for k in range(4)]
    overflow = flags[0] > 0

    places = lax.broadcasted_iota(jnp.int32, (1, voc), 1)
    vocab = jnp.concatenate([shard * voc + places, partner * voc + places], 1)
    def all_rows():
        ids = jnp.concatenate([token_ids, other_ids], 0)
        rows = jnp.concatenate([jnp.where(section == 0, pieces[0, b], pieces[1, b]) for b in (0, 1)], 0)
        return full_embedding(rows, ids, shard, vocab, (second & 1) * (width - HALF))

    start_total = lax.cond(
        overflow,
        all_rows,
        lambda: jnp.zeros((2 * voc, HALF), jnp.float32),
    )

    lower, upper = join(plane[0], plane[1], largest, *plane[2:]), join(plane[2], plane[3], largest, plane[1])
    before, behind = [send(lower, last_pairs(1))], [send(upper, last_pairs(-1))]
    total = add_products(start_total, [(weights[0][0], lower), (weights[0][1], upper)])
    late_lower, late_upper = again(upper, lower, upper)
    before.append(send(late_upper, last_pairs(1)))
    behind.append(send(late_lower, last_pairs(-1)))
    far = send(before[0], last_pairs(1)), send(behind[0], last_pairs(-1))
    total = add_products(total, [(weights[3][0], before[0]), (weights[1][1], behind[0])])
    total = add_products(total, [(weights[3][1], before[1]), (weights[1][0], behind[1])])
    total = add_products(total, [(weights[2][0], far[0]), (weights[2][1], far[1])])

    most = 6.0 * 2 * 64 * tokens
    bound = most * (largest + (flags[1:] > 0).astype(jnp.float32))
    bound = jnp.where(jnp.logical_or(overflow, bound <= 0), 2 * most, bound)
    scale = 32768.0 / bound

    sent = {}
    for a, b, p in ((1, 0, 0), (1, 1, 0), (1, 0, 1), (1, 1, 1), (0, 0, 1), (0, 1, 1), (0, 1, 0), (0, 0, 0)):
        row = p * voc + (2 * (section ^ a) + (rep ^ b)) * part
        block = lax.dynamic_slice_in_dim(total, row, part, 0)
        if a or p:
            block = (block * scale[p]).astype(jnp.float16)
        table_of = pair_pairs(a, b) if p else quad_pairs(a, b)
        sent[a, b, p] = send(block, table_of) if (a, b, p) != (0, 0, 0) else block

    def parts_of(a, b, unscale):
        low_first = pick(rep == b, x, y) & 1 == 0
        here, there = [
            block.astype(jnp.float32) * unscale if block.dtype == jnp.float16 else block
            for block in (sent[a, b, 0], sent[a, b, 1])
        ]
        return [jnp.where(low_first, here, there), jnp.where(low_first, there, here)[:, HALF - PARTS[1] :]]

    state = (table, moment_one, moment_two)
    across = fetch((section ^ 1).reshape(1).astype(jnp.int32), state, sent[0, 1, 0])
    unscale = 1.0 / scale[0]
    near = [2 * section + rep, 2 * section + (rep ^ 1)]
    here = jnp.stack(near * 2).astype(jnp.int32)
    blocks = [parts_of(0, b, unscale) for b in (0, 1)]
    *results, unscale = adamw_pair(here, unscale.reshape(1), *blocks, list(map(in_hbm, state)), None, across[0])
    blocks = [parts_of(1, b, unscale) for b in (0, 1)]
    there = jnp.stack([2 * (section ^ 1) + rep, 2 * (section ^ 1) + (rep ^ 1), rep, rep ^ 1]).astype(jnp.int32)
    return tuple(adamw_pair(there, 1.0 / scale[:1], *blocks, across, results)[:3])


def solution(mesh):
    rows = P(("shard", "section", "rep"), None)
    return jax.shard_map(
        local,
        mesh=mesh,
        in_specs=(P("section", "rep", "shard", None), P("rep", None, "shard"), P("rep", None), rows, rows, rows),
        out_specs=(rows, rows, rows),
        check_vma=False,
    )
```
